32 devices in a mesh: req: 8 (over y, x, core), tp: 4 (over z).
Axes of the slice: x: 2, y: 2, z: 4, core: 2. Of those that a mesh axis runs over, the one named last changes fastest.
Arguments:
- tokens: bfloat16 [64, 2048], P('req'), may hold values from -6 to 6
- first_gain: float32 [2048], replicated, may hold values from 0.1 to 1.9
- query_weight: bfloat16 [2048, 2048], P(None, 'tp'), may hold values from -0.125 to 0.125
- key_weight: bfloat16 [2048, 2048], P(None, 'tp'), may hold values from -0.125 to 0.125
- value_weight: bfloat16 [2048, 2048], P(None, 'tp'), may hold values from -0.125 to 0.125
- out_weight: bfloat16 [2048, 2048], P('tp'), may hold values from -0.125 to 0.125
- second_gain: float32 [2048], replicated, may hold values from 0.1 to 1.9
- up_weight: bfloat16 [2048, 8192], P(None, ('req', 'tp')), may hold values from -0.125 to 0.125
- down_weight: bfloat16 [8192, 2048], P(('req', 'tp')), may hold values from -0.0625 to 0.0625
- cache_keys: bfloat16 [32768, 2048], P('req', 'tp'), may hold values from -480 to 480
- cache_values: bfloat16 [32768, 2048], P('req', 'tp'), may hold values from -6 to 6
- lengths: int32 [64], replicated, may hold values from 1 to 8192, 32768 in all
- stream_order: int32 [64], replicated, may hold values from 0 to 63, each once
Outputs:
- hidden: bfloat16 [64, 2048], P('req', 'tp')
- new_keys: bfloat16 [64, 2048], P('req', 'tp')
- new_values: bfloat16 [64, 2048], P('req', 'tp')
The draws below stay inside these ranges and needn't reach their ends.
Inputs may be any that keep to these rules, and one draw needn't show every extreme that they name: Every request's cache holds at least one row; the lengths sum to 32768 and the longest is exactly 8192. `stream_order`: each request appears exactly once.
All inputs are finite; a program needn't handle non-finite values.
Results may differ from the reference program's by a relative error of at most 0.0055.
The reference program's roundings to bfloat16 on the way (of `normed`, `queries`, `weights`, `attended`, `normed_two` and `activation`) count: a program that leaves them out, or rounds other values in their place, can miss the bound.
Values may be sent and summed in bfloat16 or wider, within the bound.
No kernel may reach another device: no remote copies, remote signals or barrier semaphores. Data moves between devices by JAX's collectives and lax.ppermute only.
A program may use at most 128 MiB of HBM per device.

```python
import math
import jax
import jax.numpy as jnp
import numpy as np
from jax import lax

D = 2048
HEADS = 16
HEAD_DIM = 128
FF = 8192
ROWS_DEV = 4096
REQS = 64
TOTAL = 32768
MOST = 8192
N_REQ = 8


def draw_cache_keys(key, part):
    base = jnp.clip(jax.random.normal(key, (TOTAL, D), jnp.float32), -4.0, 4.0)
    return base.astype(jnp.bfloat16)


def level_of(stream_key, extent, pieces, low, largest):
    def one(position, blocks):
        steps = jax.random.uniform(jax.random.fold_in(jax.random.fold_in(stream_key, 6), position), (blocks,), jnp.float32, low / len(pieces), largest / len(pieces))
        return jnp.repeat(jnp.exp(steps), extent[position] // blocks).reshape((-1,) + (1,) * (len(extent) - position - 1))

    level = one(*pieces[0])
    for cut in pieces[1:]:
        level = level * one(*cut)
    return level


def profile(amount, total, reach, slope):
    weights = [(1 << 20) // math.isqrt(rank ** slope) + 1 for rank in range(2, amount + 1)]
    rest, holding = total - reach - (amount - 1), [1] * (amount - 1)
    while rest > 0:
        candidates = [i for i in range(amount - 1) if holding[i] < reach]
        pool, budget = sum([weights[i] for i in candidates]), rest
        for i in candidates:
            more = min(reach - holding[i], max(1, budget * weights[i] // pool), rest)
            holding[i] = holding[i] + more
            rest = rest - more
    return np.array([reach] + holding)


def ragged(stream_key, number_of, total, bound, skew):
    if number_of == 2:
        one = jax.random.randint(stream_key, (), max(1, total - bound), min(bound, total - 1) + 1)
        return jnp.stack([one, total - one])
    sizes = jnp.asarray(profile(number_of, total, bound, skew), jnp.int32)
    couples = (number_of - 1) // 2
    donor, taker = sizes[1:1 + 2 * couples:2], sizes[2:2 + 2 * couples:2]
    slack = jnp.minimum(donor - 1, bound - taker)
    moved = jax.random.randint(jax.random.fold_in(stream_key, 1), (couples,), 0, 1 << 20) % (slack + 1)
    sizes = sizes.at[1:1 + 2 * couples:2].set(donor - moved).at[2:2 + 2 * couples:2].set(taker + moved)
    return sizes[jax.random.permutation(jax.random.fold_in(stream_key, 2), number_of)]


def gaussian(stream_key, shape, width, bound, pieces=(), held_as=jnp.bfloat16):
    entries = jax.random.normal(stream_key, shape, jnp.float32) * width
    if len(pieces) > 0:
        entries = level_of(stream_key, shape, pieces, -0.22, 0.18) * entries
    return jnp.clip(entries, min=-bound, max=bound).astype(held_as)


def setup_inputs(seed: int = 0) -> dict:
    key_list = jax.random.split(jax.random.key(seed), 14)
    tokens = gaussian(key_list[0], (REQS, D), 1.0, 6.0, ((0, 8),))
    first_gain = jnp.clip(1.0 + 0.18 * jax.random.normal(key_list[1], (D,), jnp.float32), 0.1, 1.9)
    query_weight = gaussian(key_list[2], (D, D), D ** -0.5, 0.125, ((1, 4),))
    key_weight = gaussian(key_list[3], (D, D), D ** -0.5, 0.125, ((1, 4),))
    value_weight = gaussian(key_list[4], (D, D), D ** -0.5, 0.125, ((1, 4),))
    out_weight = gaussian(key_list[5], (D, D), D ** -0.5, 0.125, ((0, 4),))
    second_gain = jnp.clip(1.0 + 0.18 * jax.random.normal(key_list[6], (D,), jnp.float32), 0.1, 1.9)
    up_weight = gaussian(key_list[7], (D, FF), D ** -0.5, 0.125, ((1, 32),))
    down_weight = gaussian(key_list[8], (FF, D), FF ** -0.5, 0.0625, ((0, 32),))
    cache_keys = draw_cache_keys(jax.random.fold_in(key_list[13], 71), 0)
    cache_values = gaussian(key_list[10], (TOTAL, D), 1.0, 6.0, ((0, 8), (1, 4)))
    lengths = ragged(key_list[11], REQS, TOTAL, MOST, 2).astype(jnp.int32)
    stream_order = jax.random.permutation(key_list[12], REQS).astype(jnp.int32)
    return {"tokens": tokens, "first_gain": first_gain, "query_weight": query_weight, "key_weight": key_weight, "value_weight": value_weight, "out_weight": out_weight, "second_gain": second_gain, "up_weight": up_weight, "down_weight": down_weight, "cache_keys": cache_keys, "cache_values": cache_values, "lengths": lengths, "stream_order": stream_order}


def layer_norm(values, gain_vector):
    center = lax.optimization_barrier(jnp.mean(values, axis=-1, keepdims=True))
    shifted = values - center
    spread = lax.optimization_barrier(jnp.mean(shifted * shifted, axis=-1, keepdims=True))
    return shifted * lax.rsqrt(spread + 1e-05) * gain_vector

def reference(tokens, first_gain, query_weight, key_weight, value_weight, out_weight, second_gain, up_weight, down_weight, cache_keys, cache_values, lengths, stream_order):
    residual = tokens.astype(jnp.float32)
    normed = layer_norm(residual, first_gain).astype(jnp.bfloat16)
    queries = (jnp.dot(normed, query_weight, preferred_element_type=jnp.float32) * HEAD_DIM ** (-0.5)).astype(jnp.bfloat16)
    new_keys = jnp.dot(normed, key_weight, preferred_element_type=jnp.float32).astype(jnp.bfloat16)
    new_values = jnp.dot(normed, value_weight, preferred_element_type=jnp.float32).astype(jnp.bfloat16)
    stream_len = jnp.take(lengths, stream_order).astype(jnp.int32)
    bounds = jnp.cumsum(stream_len).astype(jnp.int32)
    positions = jnp.arange(TOTAL, dtype=jnp.int32)
    slots = jnp.searchsorted(bounds, positions, side='right').astype(jnp.int32)
    row_owner = jnp.take(stream_order, slots).astype(jnp.int32)
    key_blocks = cache_keys.reshape(N_REQ, ROWS_DEV, D)
    value_blocks = cache_values.reshape(N_REQ, ROWS_DEV, D)
    owner_blocks = row_owner.reshape(N_REQ, ROWS_DEV)

    def one_block(items):
        block_keys, block_values, block_owner = items
        row_query = jnp.take(queries, block_owner, axis=0).astype(jnp.float32).reshape(ROWS_DEV, HEADS, HEAD_DIM)
        scores = lax.optimization_barrier(jnp.sum(row_query * block_keys.astype(jnp.float32).reshape(ROWS_DEV, HEADS, HEAD_DIM), axis=-1))
        peak = jnp.maximum(jax.ops.segment_max(scores, block_owner, num_segments=REQS), -1e+30)
        expo = jnp.exp(scores - jnp.take(peak, block_owner, axis=0))
        mass = jax.ops.segment_sum(expo, block_owner, num_segments=REQS)
        weights = expo.astype(jnp.bfloat16)
        weighted = weights.astype(jnp.float32)[:, :, None] * block_values.astype(jnp.float32).reshape(ROWS_DEV, HEADS, HEAD_DIM)
        partial_value = jax.ops.segment_sum(weighted, block_owner, num_segments=REQS)
        return (peak, mass, partial_value)
    peaks, masses, partials = lax.map(one_block, (key_blocks, value_blocks, owner_blocks))
    self_score = lax.optimization_barrier(jnp.sum(queries.astype(jnp.float32).reshape(REQS, HEADS, HEAD_DIM) * new_keys.astype(jnp.float32).reshape(REQS, HEADS, HEAD_DIM), axis=-1))
    ceiling = jnp.maximum(lax.optimization_barrier(jnp.max(peaks, axis=0)), self_score)
    block_scale = jnp.exp(peaks - ceiling[None])
    self_weight = jnp.exp(self_score - ceiling)
    total = self_weight + lax.optimization_barrier(jnp.sum(masses * block_scale, axis=0))
    summed = self_weight[:, :, None] * new_values.astype(jnp.float32).reshape(REQS, HEADS, HEAD_DIM)
    summed = summed + lax.optimization_barrier(jnp.sum(partials * block_scale[:, :, :, None], axis=0))
    attended = (summed / total[:, :, None]).reshape(REQS, D).astype(jnp.bfloat16)
    middle = residual + jnp.dot(attended, out_weight, preferred_element_type=jnp.float32)
    normed_two = layer_norm(middle, second_gain).astype(jnp.bfloat16)
    activation = jax.nn.gelu(jnp.dot(normed_two, up_weight, preferred_element_type=jnp.float32), approximate=False).astype(jnp.bfloat16)
    hidden = (middle + jnp.dot(activation, down_weight, preferred_element_type=jnp.float32)).astype(jnp.bfloat16)
    return (hidden, new_keys, new_values)
```

```python
import functools

import jax
import jax.numpy as jnp
from jax import lax
from jax.experimental import pallas as pl
from jax.experimental.pallas import tpu as pltpu
from jax.sharding import PartitionSpec as P

HEAD_DIM = 128
STATS = 128
NONE = -1e30
CHUNK = 1024
MIB = 1 << 20
VMEM = pl.BlockSpec(memory_space=pltpu.VMEM)
ANY = pl.BlockSpec(memory_space=pl.ANY)
F32 = jnp.float32
BF16 = jnp.bfloat16


def layer_norm(values, gain_vector):
    center = jnp.mean(values, axis=-1, keepdims=True)
    shifted = values - center
    spread = jnp.mean(shifted * shifted, axis=-1, keepdims=True)
    return shifted * lax.rsqrt(spread + 1e-05) * gain_vector


def dot(a, b):
    return jnp.dot(a, b, preferred_element_type=F32)


def stream_ranges(lens_row, order_row):
    n = lens_row.shape[1]
    down = lax.broadcasted_iota(jnp.int32, (n, n), 0)
    across = lax.broadcasted_iota(jnp.int32, (n, n), 1)
    lens = lens_row.astype(F32)
    eye = down == across
    lens_col = jnp.sum(jnp.where(eye, lens, 0.0), axis=1, keepdims=True)
    holds = order_row == down
    slot_len = jnp.sum(jnp.where(holds, lens_col, 0.0), axis=0, keepdims=True)
    slot_len_col = jnp.sum(jnp.where(eye, slot_len, 0.0), axis=1, keepdims=True)
    before = jnp.sum(jnp.where(down < across, slot_len_col, 0.0), axis=0, keepdims=True)
    first = jnp.sum(jnp.where(holds, before, 0.0), axis=1, keepdims=True)
    return first.astype(jnp.int32), (first + lens_col).astype(jnp.int32)


def attention_kernel(
    tokens_ref,
    gain_ref,
    lens_ref,
    order_ref,
    wq_hbm,
    wk_hbm,
    wv_hbm,
    keys_hbm,
    values_hbm,
    send_ref,
    new_keys_ref,
    new_values_ref,
    self_ref,
    wq,
    wk,
    wv,
    keys,
    values,
    scores,
    own,
    sems,
):
    requests = tokens_ref.shape[0]
    rows, head_width = keys.shape
    heads = head_width // HEAD_DIM
    chunks = rows // CHUNK
    parts, own_rows, _ = send_ref.shape
    me = lax.axis_index("req")

    def piece(ref, c):
        return ref.at[pl.ds(c * CHUNK, CHUNK)]

    copies = [pltpu.make_async_copy(wq_hbm, wq, sems.at[0])]
    copies += [
        pltpu.make_async_copy(piece(keys_hbm, c), piece(keys, c), sems.at[1 + c])
        for c in range(chunks)
    ]
    copies += [
        pltpu.make_async_copy(piece(values_hbm, c), piece(values, c), sems.at[1 + chunks + c])
        for c in range(chunks)
    ]
    copies.append(pltpu.make_async_copy(wk_hbm, wk, sems.at[1 + 2 * chunks]))
    copies.append(pltpu.make_async_copy(wv_hbm, wv, sems.at[2 + 2 * chunks]))
    for copy in copies:
        copy.start()
    normed = layer_norm(tokens_ref[...].astype(F32), gain_ref[...]).astype(BF16)
    first, last = stream_ranges(lens_ref[...], order_ref[...])
    first, last = first - me * rows, last - me * rows
    copies[0].wait()
    queries = (dot(normed, wq[...]) * HEAD_DIM ** (-0.5)).astype(BF16)

    lane_max = [jnp.full((requests, 128), NONE, F32)] * heads
    for c in range(chunks):
        copies[1 + c].wait()
        place = c * CHUNK + lax.broadcasted_iota(jnp.int32, (requests, CHUNK), 1)
        member = (place >= first) & (place < last)
        for h in range(heads):
            cols = slice(h * HEAD_DIM, (h + 1) * HEAD_DIM)
            score = lax.dot_general(
                queries[:, cols],
                keys[c * CHUNK : (c + 1) * CHUNK, cols],
                (((1,), (1,)), ((), ())),
                preferred_element_type=F32,
            )
            score = jnp.where(member, score, NONE)
            scores[h, :, c * CHUNK : (c + 1) * CHUNK] = score
            for t in range(CHUNK // 128):
                lane_max[h] = jnp.maximum(lane_max[h], score[:, t * 128 : (t + 1) * 128])

    peak = [jnp.max(lane_max[h], axis=1, keepdims=True) for h in range(heads)]
    mass = [jnp.zeros((requests, 128), F32)] * heads
    partial = [jnp.zeros((requests, HEAD_DIM), F32)] * heads
    for c in range(chunks):
        copies[1 + chunks + c].wait()
        for h in range(heads):
            cols = slice(h * HEAD_DIM, (h + 1) * HEAD_DIM)
            expo = jnp.exp(scores[h, :, c * CHUNK : (c + 1) * CHUNK] - peak[h])
            for t in range(CHUNK // 128):
                mass[h] = mass[h] + expo[:, t * 128 : (t + 1) * 128]
            partial[h] = partial[h] + dot(
                expo.astype(BF16), values[c * CHUNK : (c + 1) * CHUNK, cols]
            )
    lane = lax.broadcasted_iota(jnp.int32, (requests, STATS), 1)
    stats = jnp.zeros((requests, STATS), F32)
    for h in range(heads):
        stats = jnp.where(lane == h, peak[h], stats)
        stats = jnp.where(lane == heads + h, jnp.sum(mass[h], axis=1, keepdims=True), stats)
    for d in range(parts):
        r = slice(d * own_rows, (d + 1) * own_rows)
        for h in range(heads):
            send_ref[d, :, h * HEAD_DIM : (h + 1) * HEAD_DIM] = partial[h][r]
        send_ref[d, :, head_width : head_width + STATS] = stats[r]

    copies[1 + 2 * chunks].wait()
    own[0] = queries.astype(F32)
    own[1] = dot(normed, wk[...])
    copies[2 + 2 * chunks].wait()
    own[2] = dot(normed, wv[...])
    mine = pl.ds(pl.multiple_of(me * own_rows, own_rows), own_rows)
    new_keys = own[1, mine].astype(BF16)
    new_keys_ref[...] = new_keys
    new_values_ref[...] = own[2, mine].astype(BF16)
    product = own[0, mine] * new_keys.astype(F32)
    lane = lax.broadcasted_iota(jnp.int32, (own_rows, STATS), 1)
    self_score = jnp.zeros((own_rows, STATS), F32)
    for h in range(heads):
        one = jnp.sum(product[:, h * HEAD_DIM : (h + 1) * HEAD_DIM], axis=1, keepdims=True)
        self_score = jnp.where(lane == h, one, self_score)
    self_ref[...] = self_score


def attend(tokens, gain, lens, order, wq, wk, wv, keys, values, parts):
    requests, width = tokens.shape
    rows, head_width = keys.shape
    own_rows = requests // parts
    chunks = rows // CHUNK
    return pl.pallas_call(
        attention_kernel,
        out_shape=(
            jax.ShapeDtypeStruct((parts, own_rows, head_width + STATS), F32),
            jax.ShapeDtypeStruct((own_rows, head_width), BF16),
            jax.ShapeDtypeStruct((own_rows, head_width), BF16),
            jax.ShapeDtypeStruct((own_rows, STATS), F32),
        ),
        in_specs=[VMEM] * 4 + [ANY] * 5,
        out_specs=(VMEM,) * 4,
        scratch_shapes=[pltpu.VMEM((width, head_width), BF16)] * 3
        + [pltpu.VMEM((rows, head_width), BF16)] * 2
        + [
            pltpu.VMEM((head_width // HEAD_DIM, requests, rows), F32),
            pltpu.VMEM((3, requests, head_width), F32),
            pltpu.SemaphoreType.DMA((3 + 2 * chunks,)),
        ],
        compiler_params=pltpu.CompilerParams(vmem_limit_bytes=52 * MIB),
        name="attention",
    )(tokens, gain, lens, order, wq, wk, wv, keys, values)


def merge_kernel(recv_ref, self_ref, new_values_ref, wo_ref, out_ref):
    head_width = wo_ref.shape[0]
    heads = head_width // HEAD_DIM
    attended = []
    for h in range(heads):
        cols = slice(h * HEAD_DIM, (h + 1) * HEAD_DIM)
        peak = recv_ref[:, :, head_width + h : head_width + h + 1]
        mass = recv_ref[:, :, head_width + heads + h : head_width + heads + h + 1]
        self_score = self_ref[:, h : h + 1]
        top = jnp.maximum(jnp.max(peak, axis=0), self_score)
        scale = jnp.exp(peak - top[None])
        self_weight = jnp.exp(self_score - top)
        total = self_weight + jnp.sum(scale * mass, axis=0)
        summed = self_weight * new_values_ref[:, cols].astype(F32) + jnp.sum(
            scale * recv_ref[:, :, cols], axis=0
        )
        attended.append((summed / total).astype(BF16))
    out_ref[...] = dot(jnp.concatenate(attended, axis=1), wo_ref[...])


def merge(recv, self_score, new_values, wo):
    return pl.pallas_call(
        merge_kernel,
        out_shape=jax.ShapeDtypeStruct((recv.shape[1], wo.shape[1]), F32),
        in_specs=[VMEM] * 4,
        out_specs=VMEM,
        compiler_params=pltpu.CompilerParams(vmem_limit_bytes=16 * MIB),
        name="merge",
    )(recv, self_score, new_values, wo)


def middle_kernel(parts_ref, tokens_ref, gain_ref, normed_ref, columns_ref, mid):
    tp_count = parts_ref.shape[0]
    column_width = columns_ref.shape[1]
    total = parts_ref[0].astype(F32)
    for k in range(1, tp_count):
        total = total + parts_ref[k].astype(F32)
    middle = tokens_ref[...].astype(F32) + total
    mid[...] = middle
    normed_ref[...] = layer_norm(middle, gain_ref[...]).astype(BF16)
    offset = pl.multiple_of(lax.axis_index("tp") * column_width, column_width)
    columns_ref[...] = mid[:, pl.ds(offset, column_width)]


def middle(parts, tokens, gain):
    own_rows, width = tokens.shape
    return pl.pallas_call(
        middle_kernel,
        out_shape=(
            jax.ShapeDtypeStruct((own_rows, width), BF16),
            jax.ShapeDtypeStruct((own_rows, width // parts.shape[0]), F32),
        ),
        in_specs=[VMEM] * 3,
        out_specs=(VMEM,) * 2,
        scratch_shapes=[pltpu.VMEM((own_rows, width), F32)],
        compiler_params=pltpu.CompilerParams(vmem_limit_bytes=16 * MIB),
        name="middle",
    )(parts, tokens, gain)


def mlp_kernel(normed_ref, up_ref, down_ref, out_ref):
    blocks, own_rows, column_width = out_ref.shape
    req_count = normed_ref.shape[0] // own_rows
    tp_count = blocks // req_count
    up = dot(normed_ref[...], up_ref[...])
    activation = (0.5 * up * (1.0 + lax.erf(up * 0.5**0.5))).astype(BF16)
    for t in range(tp_count):
        term = dot(activation, down_ref[:, t * column_width : (t + 1) * column_width])
        for a in range(req_count):
            out_ref[a * tp_count + t] = term[a * own_rows : (a + 1) * own_rows].astype(
                out_ref.dtype
            )


def mlp(normed, up, down, req_count, tp_count):
    requests, width = normed.shape
    return pl.pallas_call(
        mlp_kernel,
        out_shape=jax.ShapeDtypeStruct(
            (req_count * tp_count, requests // req_count, width // tp_count), BF16
        ),
        in_specs=[VMEM] * 3,
        out_specs=VMEM,
        compiler_params=pltpu.CompilerParams(vmem_limit_bytes=16 * MIB),
        name="mlp",
    )(normed, up, down)


def finish_kernel(recv_ref, columns_ref, out_ref):
    total = recv_ref[0].astype(F32)
    for k in range(1, recv_ref.shape[0]):
        total = total + recv_ref[k].astype(F32)
    out_ref[...] = (columns_ref[...] + total).astype(BF16)


def finish(recv, columns):
    return pl.pallas_call(
        finish_kernel,
        out_shape=jax.ShapeDtypeStruct(columns.shape, BF16),
        in_specs=[VMEM] * 2,
        out_specs=VMEM,
        compiler_params=pltpu.CompilerParams(vmem_limit_bytes=16 * MIB),
        name="finish",
    )(recv, columns)


def body(
    tokens,
    first_gain,
    query_weight,
    key_weight,
    value_weight,
    out_weight,
    second_gain,
    up_weight,
    down_weight,
    cache_keys,
    cache_values,
    lengths,
    stream_order,
):
    req_count = lax.axis_size("req")
    tp_count = lax.axis_size("tp")
    all_tokens = lax.all_gather(tokens, "req", axis=0, tiled=True)
    send, new_keys, new_values, self_score = attend(
        all_tokens,
        first_gain[None],
        lengths[None],
        stream_order[None],
        query_weight,
        key_weight,
        value_weight,
        cache_keys,
        cache_values,
        req_count,
    )
    recv = lax.all_to_all(send, "req", split_axis=0, concat_axis=0, tiled=True)
    part = merge(recv, self_score, new_values, out_weight)
    parts = lax.all_gather(part, "tp", axis=0)
    normed, columns = middle(parts, tokens, second_gain[None])
    all_normed = lax.all_gather(normed, "req", axis=0, tiled=True)
    term = mlp(all_normed, up_weight, down_weight, req_count, tp_count)
    terms = lax.all_to_all(term, ("req", "tp"), split_axis=0, concat_axis=0, tiled=True)
    hidden = finish(terms, columns)
    return (hidden, new_keys, new_values)


def solution(mesh):
    return jax.shard_map(
        body,
        mesh=mesh,
        in_specs=(
            P("req", None),
            P(),
            P(None, "tp"),
            P(None, "tp"),
            P(None, "tp"),
            P("tp", None),
            P(),
            P(None, ("req", "tp")),
            P(("req", "tp"), None),
            P("req", "tp"),
            P("req", "tp"),
            P(),
            P(),
        ),
        out_specs=(P("req", "tp"), P("req", "tp"), P("req", "tp")),
        check_vma=False,
    )
```

```python
import functools

import jax
import jax.numpy as jnp
from jax import lax
from jax.experimental import pallas as pl
from jax.experimental.pallas import tpu as pltpu
from jax.sharding import PartitionSpec as P

HEAD_DIM = 128
STATS = 128
NONE = -1e30
CHUNK = 1024
MIB = 1 << 20
LIMIT = 8
VMEM = pl.BlockSpec(memory_space=pltpu.VMEM)
ANY = pl.BlockSpec(memory_space=pl.ANY)
F32 = jnp.float32
BF16 = jnp.bfloat16


def layer_norm(values, gain_vector):
    center = jnp.mean(values, axis=-1, keepdims=True)
    shifted = values - center
    spread = jnp.mean(shifted * shifted, axis=-1, keepdims=True)
    return shifted * lax.rsqrt(spread + 1e-05) * gain_vector


def dot(a, b):
    return jnp.dot(a, b, preferred_element_type=F32)


def stream_ranges(lens_row, order_row):
    n = lens_row.shape[1]
    down = lax.broadcasted_iota(jnp.int32, (n, n), 0)
    across = lax.broadcasted_iota(jnp.int32, (n, n), 1)
    lens = lens_row.astype(F32)
    eye = down == across
    lens_col = jnp.sum(jnp.where(eye, lens, 0.0), axis=1, keepdims=True)
    holds = order_row == down
    slot_len = jnp.sum(jnp.where(holds, lens_col, 0.0), axis=0, keepdims=True)
    slot_len_col = jnp.sum(jnp.where(eye, slot_len, 0.0), axis=1, keepdims=True)
    before = jnp.sum(jnp.where(down < across, slot_len_col, 0.0), axis=0, keepdims=True)
    first = jnp.sum(jnp.where(holds, before, 0.0), axis=1, keepdims=True)
    return first.astype(jnp.int32), (first + lens_col).astype(jnp.int32)


def swap(x, axis, offset):
    n = lax.axis_size(axis)
    return lax.ppermute(x, axis, [(i, i ^ offset) for i in range(n)])


def exchange_order(n):
    return list(range(0, n, 2)) + list(range(1, n, 2))


def gather_far(x):
    return [swap(x, "req", m) for m in range(2, lax.axis_size("req"), 2)]


def gather_near(x, far):
    return [x[None]] + [part[None] for part in far] + [swap(jnp.stack([x] + far), "req", 1)]


def scatter_req(groups):
    n = lax.axis_size("req")
    got = [groups[0]] + [swap(groups[c], "req", 2 * c) for c in range(1, n // 2)]
    return got + [swap(jnp.stack([part[1] for part in got]), "req", 1)]


def landed_blocks(n):
    return [(c, 0) for c in range(n // 2)] + [(n // 2, c) for c in range(n // 2)]


def stacked(refs):
    blocks = [ref[k].astype(F32) for ref in refs for k in range(ref.shape[0])]
    return jnp.concatenate(blocks, axis=0)


def load_kernel(*refs):
    n = 8
    sources, targets = refs[:n], refs[n : 2 * n - 2]
    bounds_ref, lens, order, sems = refs[2 * n - 2 :]
    targets = (lens, order) + targets
    copies = [
        pltpu.make_async_copy(source, target, sems.at[k])
        for k, (source, target) in enumerate(zip(sources, targets))
    ]
    for copy in copies:
        copy.start()
    copies[0].wait()
    copies[1].wait()
    first, last = stream_ranges(lens[...], order[...])
    bounds_ref[0] = jnp.broadcast_to(first, bounds_ref.shape[1:])
    bounds_ref[1] = jnp.broadcast_to(last, bounds_ref.shape[1:])
    for copy in copies[2:]:
        copy.wait()


def load(lens, order, *arrays):
    sources = [pltpu.with_memory_space_constraint(x, pltpu.HBM) for x in (lens, order) + arrays]
    return pl.pallas_call(
        load_kernel,
        out_shape=[pltpu.VMEM(x.shape, x.dtype) for x in arrays]
        + [pltpu.VMEM((2, lens.shape[1], 128), jnp.int32)],
        in_specs=[ANY] * len(sources),
        out_specs=[VMEM] * (len(arrays) + 1),
        scratch_shapes=[
            pltpu.VMEM(lens.shape, jnp.int32),
            pltpu.VMEM(order.shape, jnp.int32),
            pltpu.SemaphoreType.DMA((len(sources),)),
        ],
        compiler_params=pltpu.CompilerParams(vmem_limit_bytes=LIMIT * MIB),
        cost_estimate=pl.CostEstimate(
            flops=0, bytes_accessed=2 * sum(x.size for x in arrays), transcendentals=0
        ),
        name="load",
    )(*sources)


def attention_kernel(req_count, n_tokens, *refs):
    token_refs, refs = refs[:n_tokens], refs[n_tokens:]
    gain_ref, bounds, wq, wk, wv, keys, values_hbm = refs[:7]
    groups = req_count // 2
    send_refs, refs = refs[7 : 7 + groups], refs[7 + groups :]
    new_keys_ref, new_values_ref, self_ref, values, scores, sems = refs
    rows, head_width = keys.shape
    heads = head_width // HEAD_DIM
    chunks = rows // CHUNK
    own_rows = new_keys_ref.shape[0]
    requests = own_rows * req_count
    me = lax.axis_index("req")

    copies = []
    for c in range(chunks):
        part = pl.ds(c * CHUNK, CHUNK)
        copies.append(pltpu.make_async_copy(values_hbm.at[part], values.at[part], sems.at[c]))
    for copy in copies:
        copy.start()
    normed = layer_norm(stacked(token_refs), gain_ref[...]).astype(BF16)
    owners = [
        pl.ds(pl.multiple_of((me ^ offset) * own_rows, own_rows), own_rows)
        for offset in exchange_order(req_count)
    ]
    first = jnp.concatenate([bounds[0, owner][:, :1] for owner in owners], axis=0) - me * rows
    last = jnp.concatenate([bounds[1, owner][:, :1] for owner in owners], axis=0) - me * rows
    queries = (dot(normed, wq[...]) * HEAD_DIM ** (-0.5)).astype(BF16)

    lane_max = [jnp.full((requests, 128), NONE, F32)] * heads
    for c in range(chunks):
        place = c * CHUNK + lax.broadcasted_iota(jnp.int32, (requests, CHUNK), 1)
        member = (place >= first) & (place < last)
        for h in range(heads):
            cols = slice(h * HEAD_DIM, (h + 1) * HEAD_DIM)
            score = lax.dot_general(
                queries[:, cols],
                keys[c * CHUNK : (c + 1) * CHUNK, cols],
                (((1,), (1,)), ((), ())),
                preferred_element_type=F32,
            )
            score = jnp.where(member, score, NONE)
            scores[h, :, c * CHUNK : (c + 1) * CHUNK] = score
            for t in range(CHUNK // 128):
                lane_max[h] = jnp.maximum(lane_max[h], score[:, t * 128 : (t + 1) * 128])

    peak = [jnp.max(lane_max[h], axis=1, keepdims=True) for h in range(heads)]
    mass = [jnp.zeros((requests, 128), F32)] * heads
    partial = [jnp.zeros((requests, HEAD_DIM), F32)] * heads
    for c in range(chunks):
        copies[c].wait()
        for h in range(heads):
            cols = slice(h * HEAD_DIM, (h + 1) * HEAD_DIM)
            expo = jnp.exp(scores[h, :, c * CHUNK : (c + 1) * CHUNK] - peak[h])
            for t in range(CHUNK // 128):
                mass[h] = mass[h] + expo[:, t * 128 : (t + 1) * 128]
            partial[h] = partial[h] + dot(
                expo.astype(BF16), values[c * CHUNK : (c + 1) * CHUNK, cols]
            )
    lane = lax.broadcasted_iota(jnp.int32, (requests, STATS), 1)
    stats = jnp.zeros((requests, STATS), F32)
    for h in range(heads):
        stats = jnp.where(lane == h, peak[h], stats)
        stats = jnp.where(lane == heads + h, jnp.sum(mass[h], axis=1, keepdims=True), stats)
    for c, ref in enumerate(send_refs):
        for k, block in enumerate((c, groups + c)):
            r = slice(block * own_rows, (block + 1) * own_rows)
            for h in range(heads):
                ref[k, :, h * HEAD_DIM : (h + 1) * HEAD_DIM] = partial[h][r]
            ref[k, :, head_width : head_width + STATS] = stats[r]

    mine = normed[: max(own_rows, 16)]
    new_keys = dot(mine, wk[...])[:own_rows].astype(BF16)
    new_values = dot(mine, wv[...])[:own_rows].astype(BF16)
    new_keys_ref[...] = new_keys
    new_values_ref[...] = new_values
    product = queries[: max(own_rows, 16)].astype(F32)[:own_rows] * new_keys.astype(F32)
    lane = lax.broadcasted_iota(jnp.int32, (own_rows, STATS), 1)
    self_score = jnp.zeros((own_rows, STATS), F32)
    for h in range(heads):
        one = jnp.sum(product[:, h * HEAD_DIM : (h + 1) * HEAD_DIM], axis=1, keepdims=True)
        self_score = jnp.where(lane == h, one, self_score)
    self_ref[:, :head_width] = new_values.astype(F32)
    self_ref[:, head_width:] = self_score


def attend(tokens, gain, bounds, wq, wk, wv, keys, values):
    req_count = lax.axis_size("req")
    own_rows, width = tokens[0].shape[1:]
    requests = own_rows * req_count
    rows, head_width = keys.shape
    heads = head_width // HEAD_DIM
    groups = req_count // 2
    *sends, new_keys, new_values, self_part = pl.pallas_call(
        functools.partial(attention_kernel, req_count, len(tokens)),
        out_shape=[jax.ShapeDtypeStruct((2, own_rows, head_width + STATS), F32)] * groups
        + [jax.ShapeDtypeStruct((own_rows, head_width), BF16)] * 2
        + [jax.ShapeDtypeStruct((own_rows, head_width + STATS), F32)],
        in_specs=[VMEM] * (len(tokens) + 6) + [ANY],
        out_specs=[VMEM] * (groups + 3),
        scratch_shapes=[
            pltpu.VMEM((rows, head_width), BF16),
            pltpu.VMEM((heads, requests, rows), F32),
            pltpu.SemaphoreType.DMA((rows // CHUNK,)),
        ],
        compiler_params=pltpu.CompilerParams(vmem_limit_bytes=heads * requests * rows * 4 + (4 + LIMIT) * MIB),
        name="attention",
    )(
        *tokens,
        gain,
        bounds,
        wq,
        wk,
        wv,
        keys,
        pltpu.with_memory_space_constraint(values, pltpu.HBM),
    )
    return sends, new_keys, new_values, self_part


def merge_kernel(places, n_landed, *refs):
    landed, (self_ref, wo_ref, part_ref, sent_ref) = refs[:n_landed], refs[n_landed:]
    head_width = wo_ref.shape[0]
    heads = head_width // HEAD_DIM
    attended = []
    for h in range(heads):
        cols = slice(h * HEAD_DIM, (h + 1) * HEAD_DIM)
        at_peak = slice(head_width + h, head_width + h + 1)
        at_mass = slice(head_width + heads + h, head_width + heads + h + 1)
        self_score = self_ref[:, at_peak]
        peaks = [landed[a][k, :, at_peak] for a, k in places]
        top = functools.reduce(jnp.maximum, peaks, self_score)
        total = jnp.exp(self_score - top)
        summed = total * self_ref[:, cols]
        for (a, k), peak in zip(places, peaks):
            scale = jnp.exp(peak - top)
            total = total + scale * landed[a][k, :, at_mass]
            summed = summed + scale * landed[a][k, :, cols]
        attended.append((summed / total).astype(BF16))
    part = dot(jnp.concatenate(attended, axis=1), wo_ref[...])
    part_ref[...] = part
    sent_ref[...] = part.astype(BF16)


def merge(landed, self_part, wo):
    shape = (self_part.shape[0], wo.shape[1])
    return pl.pallas_call(
        functools.partial(merge_kernel, landed_blocks(lax.axis_size("req")), len(landed)),
        out_shape=(jax.ShapeDtypeStruct(shape, F32), jax.ShapeDtypeStruct(shape, BF16)),
        in_specs=[VMEM] * (len(landed) + 2),
        out_specs=(VMEM,) * 2,
        compiler_params=pltpu.CompilerParams(vmem_limit_bytes=16 * MIB),
        name="merge",
    )(*landed, self_part, wo)


def middle_kernel(*refs):
    part_ref, *others, tokens_ref, gain_ref, normed_ref, columns_ref, mid = refs
    column_width = columns_ref.shape[1]
    total = part_ref[...]
    for other in others:
        total = total + other[...].astype(F32)
    middle = tokens_ref[...].astype(F32) + total
    mid[...] = middle
    normed_ref[...] = layer_norm(middle, gain_ref[...]).astype(BF16)
    offset = pl.multiple_of(lax.axis_index("tp") * column_width, column_width)
    columns_ref[...] = mid[:, pl.ds(offset, column_width)]


def middle(part, others, tokens, gain):
    own_rows, width = tokens.shape
    return pl.pallas_call(
        middle_kernel,
        out_shape=(
            jax.ShapeDtypeStruct((own_rows, width), BF16),
            jax.ShapeDtypeStruct((own_rows, width // (1 + len(others))), F32),
        ),
        in_specs=[VMEM] * (3 + len(others)),
        out_specs=(VMEM,) * 2,
        scratch_shapes=[pltpu.VMEM((own_rows, width), F32)],
        compiler_params=pltpu.CompilerParams(vmem_limit_bytes=16 * MIB),
        name="middle",
    )(part, *others, tokens, gain)


def mlp_kernel(req_count, *refs):
    *normed_refs, up_ref, down_ref, out_ref = refs
    blocks, own_rows, column_width = out_ref.shape
    tp_count = blocks // req_count
    me = lax.axis_index("req")
    up = dot(stacked(normed_refs).astype(BF16), up_ref[...])
    activation = (0.5 * up * (1.0 + lax.erf(up * 0.5**0.5))).astype(BF16)
    for t in range(tp_count):
        term = dot(activation, down_ref[:, t * column_width : (t + 1) * column_width])
        for k, offset in enumerate(exchange_order(req_count)):
            out_ref[(me ^ offset) * tp_count + t] = term[
                k * own_rows : (k + 1) * own_rows
            ].astype(BF16)


def mlp(normed, up, down):
    req_count, tp_count = lax.axis_size("req"), lax.axis_size("tp")
    own_rows, width = normed[0].shape[1:]
    return pl.pallas_call(
        functools.partial(mlp_kernel, req_count),
        out_shape=jax.ShapeDtypeStruct(
            (req_count * tp_count, own_rows, width // tp_count), BF16
        ),
        in_specs=[VMEM] * (len(normed) + 2),
        out_specs=VMEM,
        compiler_params=pltpu.CompilerParams(vmem_limit_bytes=16 * MIB),
        name="mlp",
    )(*normed, up, down)


def finish_kernel(recv_ref, columns_ref, out_ref):
    total = recv_ref[0].astype(F32)
    for k in range(1, recv_ref.shape[0]):
        total = total + recv_ref[k].astype(F32)
    out_ref[...] = (columns_ref[...] + total).astype(BF16)


def finish(recv, columns):
    return pl.pallas_call(
        finish_kernel,
        out_shape=jax.ShapeDtypeStruct(columns.shape, BF16),
        in_specs=[VMEM] * 2,
        out_specs=VMEM,
        compiler_params=pltpu.CompilerParams(vmem_limit_bytes=16 * MIB),
        name="finish",
    )(recv, columns)


def body(
    tokens,
    first_gain,
    query_weight,
    key_weight,
    value_weight,
    out_weight,
    second_gain,
    up_weight,
    down_weight,
    cache_keys,
    cache_values,
    lengths,
    stream_order,
):
    far = gather_far(tokens)
    tokens, gain, wq, wk, wv, keys, bounds = load(
        lengths[None],
        stream_order[None],
        tokens,
        first_gain[None],
        query_weight,
        key_weight,
        value_weight,
        cache_keys,
    )
    sends, new_keys, new_values, self_part = attend(
        gather_near(tokens, far), gain, bounds, wq, wk, wv, keys, cache_values
    )
    part, sent = merge(scatter_req(sends), self_part, out_weight)
    others = [swap(sent, "tp", m) for m in range(1, lax.axis_size("tp"))]
    normed, columns = middle(part, others, tokens, second_gain[None])
    term = mlp(gather_near(normed, gather_far(normed)), up_weight, down_weight)
    terms = lax.all_to_all(term, ("req", "tp"), split_axis=0, concat_axis=0, tiled=True)
    hidden = finish(terms, columns)
    return (hidden, new_keys, new_values)


def solution(mesh):
    return jax.shard_map(
        body,
        mesh=mesh,
        in_specs=(
            P("req", None),
            P(),
            P(None, "tp"),
            P(None, "tp"),
            P(None, "tp"),
            P("tp", None),
            P(),
            P(None, ("req", "tp")),
            P(("req", "tp"), None),
            P("req", "tp"),
            P("req", "tp"),
            P(),
            P(),
        ),
        out_specs=(P("req", "tp"), P("req", "tp"), P("req", "tp")),
        check_vma=False,
    )
```

```python
import functools

import jax
import jax.numpy as jnp
from jax import lax
from jax.experimental import pallas as pl
from jax.experimental.pallas import tpu as pltpu
from jax.sharding import PartitionSpec as P

HEAD_DIM = 128
STATS = 128
NONE = -1e30
CHUNK = 1024
MIB = 1 << 20
LIMIT = 8
VMEM = pl.BlockSpec(memory_space=pltpu.VMEM)
ANY = pl.BlockSpec(memory_space=pl.ANY)
F32 = jnp.float32
BF16 = jnp.bfloat16


def layer_norm(values, gain_vector):
    center = jnp.mean(values, axis=-1, keepdims=True)
    shifted = values - center
    spread = jnp.mean(shifted * shifted, axis=-1, keepdims=True)
    return shifted * lax.rsqrt(spread + 1e-05) * gain_vector


def dot(a, b):
    return jnp.dot(a, b, preferred_element_type=F32)


def stream_ranges(lens_row, order_row):
    n = lens_row.shape[1]
    down = lax.broadcasted_iota(jnp.int32, (n, n), 0)
    across = lax.broadcasted_iota(jnp.int32, (n, n), 1)
    lens = lens_row.astype(F32)
    eye = down == across
    lens_col = jnp.sum(jnp.where(eye, lens, 0.0), axis=1, keepdims=True)
    holds = order_row == down
    slot_len = jnp.sum(jnp.where(holds, lens_col, 0.0), axis=0, keepdims=True)
    slot_len_col = jnp.sum(jnp.where(eye, slot_len, 0.0), axis=1, keepdims=True)
    before = jnp.sum(jnp.where(down < across, slot_len_col, 0.0), axis=0, keepdims=True)
    first = jnp.sum(jnp.where(holds, before, 0.0), axis=1, keepdims=True)
    return first.astype(jnp.int32), (first + lens_col).astype(jnp.int32)


def swap(x, axis, offset):
    n = lax.axis_size(axis)
    return lax.ppermute(x, axis, [(i, i ^ offset) for i in range(n)])


def exchange_order(n):
    return list(range(0, n, 2)) + list(range(1, n, 2))


def gather_far(x):
    return [swap(x, "req", m) for m in range(2, lax.axis_size("req"), 2)]


def gather_near(x, far):
    return [x[None]] + [part[None] for part in far] + [swap(jnp.stack([x] + far), "req", 1)]


def scatter_far(groups):
    return [groups[0]] + [swap(groups[c], "req", 2 * c) for c in range(1, len(groups))]


def scatter_near(near, far):
    return swap(jnp.stack([near] + [part[1] for part in far]), "req", 1)


def landed_blocks(n):
    return [(c, 0) for c in range(n // 2)] + [(n // 2, c) for c in range(n // 2)]


def split_three(x):
    parts = []
    for _ in range(3):
        parts.append(x.astype(BF16).astype(F32))
        x = x - parts[-1]
    return parts


def stacked(refs):
    blocks = [ref[k].astype(F32) for ref in refs for k in range(ref.shape[0])]
    return jnp.concatenate(blocks, axis=0)


def load_kernel(n, *refs):
    sources, targets = refs[:n], refs[n : 2 * n - 2]
    bounds_ref, lens, order, sems = refs[2 * n - 2 :]
    targets = (lens, order) + targets
    copies = [
        pltpu.make_async_copy(source.at[pl.ds(0, target.shape[0])], target, sems.at[k])
        for k, (source, target) in enumerate(zip(sources, targets))
    ]
    for copy in copies:
        copy.start()
    copies[0].wait()
    copies[1].wait()
    first, last = stream_ranges(lens[...], order[...])
    bounds_ref[0] = jnp.broadcast_to(first, bounds_ref.shape[1:])
    bounds_ref[1] = jnp.broadcast_to(last, bounds_ref.shape[1:])
    for copy in copies[2:]:
        copy.wait()


def load(lens, order, *arrays, last_rows):
    sources = [pltpu.with_memory_space_constraint(x, pltpu.HBM) for x in (lens, order) + arrays]
    last = arrays[-1]
    return pl.pallas_call(
        functools.partial(load_kernel, len(sources)),
        out_shape=[pltpu.VMEM(x.shape, x.dtype) for x in arrays[:-1]]
        + [pltpu.VMEM((last_rows, last.shape[1]), last.dtype)]
        + [pltpu.VMEM((2, lens.shape[1], 128), jnp.int32)],
        in_specs=[ANY] * len(sources),
        out_specs=[VMEM] * (len(arrays) + 1),
        scratch_shapes=[
            pltpu.VMEM(lens.shape, jnp.int32),
            pltpu.VMEM(order.shape, jnp.int32),
            pltpu.SemaphoreType.DMA((len(sources),)),
        ],
        compiler_params=pltpu.CompilerParams(vmem_limit_bytes=LIMIT * MIB),
        cost_estimate=pl.CostEstimate(
            flops=0, bytes_accessed=2 * sum(x.size for x in arrays), transcendentals=0
        ),
        name="load",
    )(*sources)


def attention_kernel(req_count, n_tokens, *refs):
    token_refs, refs = refs[:n_tokens], refs[n_tokens:]
    gain_ref, bounds, wq, first_keys, keys_hbm, values_hbm = refs[:6]
    groups = req_count // 2
    send_refs, refs = refs[6 : 6 + groups], refs[6 + groups :]
    own_normed_ref, own_queries_ref, last_keys, values, scores, sems = refs
    rows, head_width = values.shape
    held = first_keys.shape[0]
    heads = head_width // HEAD_DIM
    chunks = rows // CHUNK
    own_rows = own_normed_ref.shape[0] // 2
    requests = own_rows * req_count
    me = lax.axis_index("req")

    copies = []
    for c in range(held // CHUNK, chunks):
        there, here = pl.ds(c * CHUNK, CHUNK), pl.ds(c * CHUNK - held, CHUNK)
        copies.append(
            pltpu.make_async_copy(keys_hbm.at[there], last_keys.at[here], sems.at[len(copies)])
        )
    late = len(copies)
    for c in range(chunks):
        part = pl.ds(c * CHUNK, CHUNK)
        copies.append(
            pltpu.make_async_copy(values_hbm.at[part], values.at[part], sems.at[len(copies)])
        )
    for copy in copies:
        copy.start()
    normed = layer_norm(stacked(token_refs), gain_ref[...]).astype(BF16)
    owners = [
        pl.ds(pl.multiple_of((me ^ offset) * own_rows, own_rows), own_rows)
        for offset in exchange_order(req_count)
    ]
    first = jnp.concatenate([bounds[0, owner][:, :1] for owner in owners], axis=0) - me * rows
    last = jnp.concatenate([bounds[1, owner][:, :1] for owner in owners], axis=0) - me * rows
    queries = (dot(normed, wq[...]) * HEAD_DIM ** (-0.5)).astype(BF16)

    lane_max = [jnp.full((requests, 128), NONE, F32)] * heads
    for c in range(chunks):
        keys, at = first_keys, c * CHUNK
        if at >= held:
            copies[(at - held) // CHUNK].wait()
            keys, at = last_keys, at - held
        place = c * CHUNK + lax.broadcasted_iota(jnp.int32, (requests, CHUNK), 1)
        member = (place >= first) & (place < last)
        for h in range(heads):
            cols = slice(h * HEAD_DIM, (h + 1) * HEAD_DIM)
            score = lax.dot_general(
                queries[:, cols],
                keys[at : at + CHUNK, cols],
                (((1,), (1,)), ((), ())),
                preferred_element_type=F32,
            )
            score = jnp.where(member, score, NONE)
            scores[h, :, c * CHUNK : (c + 1) * CHUNK] = score
            for t in range(CHUNK // 128):
                lane_max[h] = jnp.maximum(lane_max[h], score[:, t * 128 : (t + 1) * 128])

    peak = [jnp.max(lane_max[h], axis=1, keepdims=True) for h in range(heads)]
    mass = [jnp.zeros((requests, 128), F32)] * heads
    partial = [jnp.zeros((requests, HEAD_DIM), F32)] * heads
    for c in range(chunks):
        copies[late + c].wait()
        for h in range(heads):
            cols = slice(h * HEAD_DIM, (h + 1) * HEAD_DIM)
            expo = jnp.exp(scores[h, :, c * CHUNK : (c + 1) * CHUNK] - peak[h])
            for t in range(CHUNK // 128):
                mass[h] = mass[h] + expo[:, t * 128 : (t + 1) * 128]
            partial[h] = partial[h] + dot(
                expo.astype(BF16), values[c * CHUNK : (c + 1) * CHUNK, cols]
            )
    lane = lax.broadcasted_iota(jnp.int32, (requests, STATS), 1)
    stats = jnp.zeros((requests, STATS), F32)
    for h in range(heads):
        both = (peak[h], jnp.sum(mass[h], axis=1, keepdims=True))
        for kind, number in enumerate(both):
            for k, piece in enumerate(split_three(number)):
                stats = jnp.where(lane == (kind * heads + h) * 3 + k, piece, stats)
    for c, ref in enumerate(send_refs):
        for k, block in enumerate((c, groups + c)):
            r = slice(block * own_rows, (block + 1) * own_rows)
            for h in range(heads):
                ref[k, :, h * HEAD_DIM : (h + 1) * HEAD_DIM] = partial[h][r].astype(BF16)
            ref[k, :, head_width : head_width + STATS] = stats[r].astype(BF16)
    own_normed_ref[...] = normed[: 2 * own_rows]
    own_queries_ref[...] = queries[: 2 * own_rows].astype(F32)


def attend(tokens, gain, bounds, wq, first_keys, keys, values):
    req_count = lax.axis_size("req")
    own_rows, width = tokens[0].shape[1:]
    requests = own_rows * req_count
    rows, head_width = keys.shape
    heads = head_width // HEAD_DIM
    groups = req_count // 2
    scratch = heads * requests * rows * 4 + 4 * rows * head_width
    *sends, own_normed, own_queries = pl.pallas_call(
        functools.partial(attention_kernel, req_count, len(tokens)),
        out_shape=[jax.ShapeDtypeStruct((2, own_rows, head_width + STATS), BF16)] * groups
        + [
            jax.ShapeDtypeStruct((2 * own_rows, width), BF16),
            jax.ShapeDtypeStruct((2 * own_rows, head_width), F32),
        ],
        in_specs=[VMEM] * (len(tokens) + 4) + [ANY] * 2,
        out_specs=[VMEM] * (groups + 2),
        scratch_shapes=[
            pltpu.VMEM((rows - first_keys.shape[0], head_width), BF16),
            pltpu.VMEM((rows, head_width), BF16),
            pltpu.VMEM((heads, requests, rows), F32),
            pltpu.SemaphoreType.DMA((2 * rows // CHUNK,)),
        ],
        compiler_params=pltpu.CompilerParams(vmem_limit_bytes=scratch + LIMIT * MIB),
        name="attention",
    )(
        *tokens,
        gain,
        bounds,
        wq,
        first_keys,
        pltpu.with_memory_space_constraint(keys, pltpu.HBM),
        pltpu.with_memory_space_constraint(values, pltpu.HBM),
    )
    return sends, own_normed, own_queries


def own_kernel(normed_ref, queries_ref, wk, wv, group_ref, new_keys_ref, new_values_ref, self_ref, near_ref):
    own_rows, head_width = new_keys_ref.shape
    new_keys = dot(normed_ref[...], wk[...])[:own_rows].astype(BF16)
    new_values = dot(normed_ref[...], wv[...])[:own_rows].astype(BF16)
    new_keys_ref[...] = new_keys
    new_values_ref[...] = new_values
    product = queries_ref[:own_rows] * new_keys.astype(F32)
    lane = lax.broadcasted_iota(jnp.int32, (own_rows, STATS), 1)
    self_score = jnp.zeros((own_rows, STATS), F32)
    for h in range(head_width // HEAD_DIM):
        one = jnp.sum(product[:, h * HEAD_DIM : (h + 1) * HEAD_DIM], axis=1, keepdims=True)
        self_score = jnp.where(lane == h, one, self_score)
    self_ref[:, :head_width] = new_values.astype(F32)
    self_ref[:, head_width:] = self_score
    near_ref[...] = group_ref[1]


def own_part(normed, queries, wk, wv, group):
    own_rows, head_width = normed.shape[0] // 2, wk.shape[1]
    return pl.pallas_call(
        own_kernel,
        out_shape=[
            jax.ShapeDtypeStruct((own_rows, head_width), BF16),
            jax.ShapeDtypeStruct((own_rows, head_width), BF16),
            jax.ShapeDtypeStruct((own_rows, head_width + STATS), F32),
            jax.ShapeDtypeStruct(group.shape[1:], BF16),
        ],
        in_specs=[VMEM] * 5,
        out_specs=[VMEM] * 4,
        compiler_params=pltpu.CompilerParams(vmem_limit_bytes=LIMIT * MIB),
        name="own",
    )(normed, queries, wk, wv, group)


def merge_kernel(places, n_landed, *refs):
    landed, (self_ref, wo_ref, part_ref, sent_ref) = refs[:n_landed], refs[n_landed:]
    head_width = wo_ref.shape[0]
    heads = head_width // HEAD_DIM
    attended = []
    for h in range(heads):
        cols = slice(h * HEAD_DIM, (h + 1) * HEAD_DIM)
        self_score = self_ref[:, head_width + h : head_width + h + 1]

        def stat(a, k, kind):
            at = head_width + (kind * heads + h) * 3
            hi, mid, lo = (
                landed[a][k, :, at + j : at + j + 1].astype(F32) for j in range(3)
            )
            return hi + mid + lo

        peaks = [stat(a, k, 0) for a, k in places]
        top = functools.reduce(jnp.maximum, peaks, self_score)
        total = jnp.exp(self_score - top)
        summed = total * self_ref[:, cols]
        for (a, k), peak in zip(places, peaks):
            scale = jnp.exp(peak - top)
            total = total + scale * stat(a, k, 1)
            summed = summed + scale * landed[a][k, :, cols].astype(F32)
        attended.append((summed / total).astype(BF16))
    part = dot(jnp.concatenate(attended, axis=1), wo_ref[...])
    part_ref[...] = part
    sent_ref[...] = part.astype(BF16)


def merge(landed, self_part, wo):
    shape = (self_part.shape[0], wo.shape[1])
    return pl.pallas_call(
        functools.partial(merge_kernel, landed_blocks(lax.axis_size("req")), len(landed)),
        out_shape=(jax.ShapeDtypeStruct(shape, F32), jax.ShapeDtypeStruct(shape, BF16)),
        in_specs=[VMEM] * (len(landed) + 2),
        out_specs=(VMEM,) * 2,
        compiler_params=pltpu.CompilerParams(vmem_limit_bytes=16 * MIB),
        name="merge",
    )(*landed, self_part, wo)


def middle_kernel(*refs):
    part_ref, *others, tokens_ref, gain_ref, normed_ref, columns_ref, mid = refs
    column_width = columns_ref.shape[1]
    total = part_ref[...]
    for other in others:
        total = total + other[...].astype(F32)
    middle = tokens_ref[...].astype(F32) + total
    mid[...] = middle
    normed_ref[...] = layer_norm(middle, gain_ref[...]).astype(BF16)
    offset = pl.multiple_of(lax.axis_index("tp") * column_width, column_width)
    columns_ref[...] = mid[:, pl.ds(offset, column_width)]


def middle(part, others, tokens, gain):
    own_rows, width = tokens.shape
    return pl.pallas_call(
        middle_kernel,
        out_shape=(
            jax.ShapeDtypeStruct((own_rows, width), BF16),
            jax.ShapeDtypeStruct((own_rows, width // (1 + len(others))), F32),
        ),
        in_specs=[VMEM] * (3 + len(others)),
        out_specs=(VMEM,) * 2,
        scratch_shapes=[pltpu.VMEM((own_rows, width), F32)],
        compiler_params=pltpu.CompilerParams(vmem_limit_bytes=16 * MIB),
        name="middle",
    )(part, *others, tokens, gain)


def mlp_kernel(req_count, tp_count, n_normed, *refs):
    normed_refs, (up_ref, down_ref, up_peer_ref, down_peer_ref, out_ref) = refs[:n_normed], refs[n_normed:]
    own_rows, column_width = out_ref.shape[1:]
    me = lax.axis_index("req")
    normed = stacked(normed_refs).astype(BF16)
    activations = []
    for ref in (up_ref, up_peer_ref):
        up = dot(normed, ref[...])
        activations.append((0.5 * up * (1.0 + lax.erf(up * 0.5**0.5))).astype(BF16))
    for t in range(tp_count):
        cols = slice(t * column_width, (t + 1) * column_width)
        term = dot(activations[0], down_ref[:, cols]) + dot(activations[1], down_peer_ref[:, cols])
        for c in range(req_count // 2):
            out_ref[((me ^ (2 * c)) // 2) * tp_count + t] = term[
                c * own_rows : (c + 1) * own_rows
            ].astype(BF16)


def mlp(normed, *weights):
    req_count, tp_count = lax.axis_size("req"), lax.axis_size("tp")
    own_rows, width = normed[0].shape[1:]
    return pl.pallas_call(
        functools.partial(mlp_kernel, req_count, tp_count, len(normed)),
        out_shape=jax.ShapeDtypeStruct(
            (req_count * tp_count // 2, own_rows, width // tp_count), BF16
        ),
        in_specs=[VMEM] * (len(normed) + len(weights)),
        out_specs=VMEM,
        compiler_params=pltpu.CompilerParams(vmem_limit_bytes=16 * MIB),
        name="mlp",
    )(*normed, *weights)


def finish_kernel(recv_ref, columns_ref, out_ref):
    total = recv_ref[0].astype(F32)
    for k in range(1, recv_ref.shape[0]):
        total = total + recv_ref[k].astype(F32)
    out_ref[...] = (columns_ref[...] + total).astype(BF16)


def finish(recv, columns):
    return pl.pallas_call(
        finish_kernel,
        out_shape=jax.ShapeDtypeStruct(columns.shape, BF16),
        in_specs=[VMEM] * 2,
        out_specs=VMEM,
        compiler_params=pltpu.CompilerParams(vmem_limit_bytes=16 * MIB),
        name="finish",
    )(recv, columns)


def body(
    tokens,
    first_gain,
    query_weight,
    key_weight,
    value_weight,
    out_weight,
    second_gain,
    up_weight,
    down_weight,
    cache_keys,
    cache_values,
    lengths,
    stream_order,
):
    req_count = lax.axis_size("req")
    tp_count = lax.axis_size("tp")
    up_peer, down_peer = swap(up_weight, "req", 1), swap(down_weight, "req", 1)
    far = gather_far(tokens)
    tokens, gain, wq, first_keys, bounds = load(
        lengths[None],
        stream_order[None],
        tokens,
        first_gain[None],
        query_weight,
        cache_keys,
        last_rows=cache_keys.shape[0] // 2,
    )
    sends, own_normed, own_queries = attend(
        gather_near(tokens, far), gain, bounds, wq, first_keys, cache_keys, cache_values
    )
    new_keys, new_values, self_part, near = own_part(
        own_normed, own_queries, key_weight, value_weight, sends[0]
    )
    landed = scatter_far(sends)
    landed.append(scatter_near(near, landed[1:]))
    part, sent = merge(landed, self_part, out_weight)
    others = [swap(sent, "tp", m) for m in range(1, tp_count)]
    normed, columns = middle(part, others, tokens, second_gain[None])
    all_normed = [part[None] for part in [normed] + gather_far(normed)]
    term = mlp(all_normed, up_weight, down_weight, up_peer, down_peer)
    same_core = [
        [i * tp_count + t for i in range(core, req_count, 2) for t in range(tp_count)]
        for core in range(2)
    ]
    terms = lax.all_to_all(
        term,
        ("req", "tp"),
        split_axis=0,
        concat_axis=0,
        tiled=True,
        axis_index_groups=same_core,
    )
    hidden = finish(terms, columns)
    return (hidden, new_keys, new_values)


def solution(mesh):
    return jax.shard_map(
        body,
        mesh=mesh,
        in_specs=(
            P("req", None),
            P(),
            P(None, "tp"),
            P(None, "tp"),
            P(None, "tp"),
            P("tp", None),
            P(),
            P(None, ("req", "tp")),
            P(("req", "tp"), None),
            P("req", "tp"),
            P("req", "tp"),
            P(),
            P(),
        ),
        out_specs=(P("req", "tp"), P("req", "tp"), P("req", "tp")),
        check_vma=False,
    )
```

```python
import functools

import jax
import jax.numpy as jnp
from jax import lax
from jax.experimental import pallas as pl
from jax.experimental.pallas import tpu as pltpu
from jax.sharding import PartitionSpec as P

HEAD_DIM = 128
STATS = 128
NONE = -1e30
CHUNK = 1024
MIB = 1 << 20
LIMIT = 8
VMEM = pl.BlockSpec(memory_space=pltpu.VMEM)
ANY = pl.BlockSpec(memory_space=pl.ANY)
F32 = jnp.float32
BF16 = jnp.bfloat16


def layer_norm(values, gain_vector):
    center = jnp.mean(values, axis=-1, keepdims=True)
    shifted = values - center
    spread = jnp.mean(shifted * shifted, axis=-1, keepdims=True)
    return shifted * lax.rsqrt(spread + 1e-05) * gain_vector


def dot(a, b):
    return jnp.dot(a, b, preferred_element_type=F32)


def stream_ranges(lens_row, order_row):
    n = lens_row.shape[1]
    down = lax.broadcasted_iota(jnp.int32, (n, n), 0)
    across = lax.broadcasted_iota(jnp.int32, (n, n), 1)
    lens = lens_row.astype(F32)
    eye = down == across
    lens_col = jnp.sum(jnp.where(eye, lens, 0.0), axis=1, keepdims=True)
    holds = order_row == down
    slot_len = jnp.sum(jnp.where(holds, lens_col, 0.0), axis=0, keepdims=True)
    slot_len_col = jnp.sum(jnp.where(eye, slot_len, 0.0), axis=1, keepdims=True)
    before = jnp.sum(jnp.where(down < across, slot_len_col, 0.0), axis=0, keepdims=True)
    first = jnp.sum(jnp.where(holds, before, 0.0), axis=1, keepdims=True)
    return first.astype(jnp.int32), (first + lens_col).astype(jnp.int32)


def swap(x, axis, offset):
    n = lax.axis_size(axis)
    return lax.ppermute(x, axis, [(i, i ^ offset) for i in range(n)])


def far_offsets(n):
    return list(range(n - 2, 0, -2))


def exchange_order(n):
    same = [0] + far_offsets(n)
    return same + [offset + 1 for offset in same]


def gather_far(x):
    return [swap(x, "req", m) for m in far_offsets(lax.axis_size("req"))]


def gather_near(x, far):
    return [x[None]] + [part[None] for part in far] + [swap(jnp.stack([x] + far), "req", 1)]


def scatter_far(groups):
    offsets = far_offsets(lax.axis_size("req"))
    return groups[:1] + [swap(group, "req", m) for group, m in zip(groups[1:], offsets)]


def scatter_near(near, far):
    return swap(jnp.stack([near] + [part[1] for part in far]), "req", 1)


def landed_blocks(n):
    return [(c, 0) for c in range(n // 2)] + [(n // 2, c) for c in range(n // 2)]


def split_three(x):
    parts = []
    for _ in range(3):
        parts.append(x.astype(BF16).astype(F32))
        x = x - parts[-1]
    return parts


def stacked(refs):
    blocks = [ref[k].astype(F32) for ref in refs for k in range(ref.shape[0])]
    return jnp.concatenate(blocks, axis=0)


def load_kernel(n, *refs):
    sources, targets = refs[:n], refs[n : 2 * n - 2]
    bounds_ref, lens, order, sems = refs[2 * n - 2 :]
    targets = (lens, order) + targets
    copies = [
        pltpu.make_async_copy(source.at[pl.ds(0, target.shape[0])], target, sems.at[k])
        for k, (source, target) in enumerate(zip(sources, targets))
    ]
    for copy in copies:
        copy.start()
    copies[0].wait()
    copies[1].wait()
    first, last = stream_ranges(lens[...], order[...])
    bounds_ref[0] = jnp.broadcast_to(first, bounds_ref.shape[1:])
    bounds_ref[1] = jnp.broadcast_to(last, bounds_ref.shape[1:])
    for copy in copies[2:]:
        copy.wait()


def load(lens, order, *arrays, last_rows):
    sources = [pltpu.with_memory_space_constraint(x, pltpu.HBM) for x in (lens, order) + arrays]
    last = arrays[-1]
    return pl.pallas_call(
        functools.partial(load_kernel, len(sources)),
        out_shape=[pltpu.VMEM(x.shape, x.dtype) for x in arrays[:-1]]
        + [pltpu.VMEM((last_rows, last.shape[1]), last.dtype)]
        + [pltpu.VMEM((2, lens.shape[1], 128), jnp.int32)],
        in_specs=[ANY] * len(sources),
        out_specs=[VMEM] * (len(arrays) + 1),
        scratch_shapes=[
            pltpu.VMEM(lens.shape, jnp.int32),
            pltpu.VMEM(order.shape, jnp.int32),
            pltpu.SemaphoreType.DMA((len(sources),)),
        ],
        compiler_params=pltpu.CompilerParams(vmem_limit_bytes=LIMIT * MIB),
        cost_estimate=pl.CostEstimate(
            flops=0, bytes_accessed=2 * sum(x.size for x in arrays), transcendentals=0
        ),
        name="load",
    )(*sources)


def attention_kernel(req_count, n_tokens, *refs):
    token_refs, refs = refs[:n_tokens], refs[n_tokens:]
    gain_ref, bounds, wq, first_keys, keys_hbm, values_hbm = refs[:6]
    groups = req_count // 2
    send_refs, refs = refs[6 : 6 + groups], refs[6 + groups :]
    own_normed_ref, own_queries_ref, last_keys, values, scores, sems = refs
    rows, head_width = values.shape
    held = first_keys.shape[0]
    heads = head_width // HEAD_DIM
    chunks = rows // CHUNK
    own_rows = own_normed_ref.shape[0] // 2
    requests = own_rows * req_count
    me = lax.axis_index("req")

    copies = []
    for c in range(held // CHUNK, chunks):
        there, here = pl.ds(c * CHUNK, CHUNK), pl.ds(c * CHUNK - held, CHUNK)
        copies.append(
            pltpu.make_async_copy(keys_hbm.at[there], last_keys.at[here], sems.at[len(copies)])
        )
    late = len(copies)
    for c in range(chunks):
        part = pl.ds(c * CHUNK, CHUNK)
        copies.append(
            pltpu.make_async_copy(values_hbm.at[part], values.at[part], sems.at[len(copies)])
        )
    for copy in copies:
        copy.start()
    normed = layer_norm(stacked(token_refs), gain_ref[...]).astype(BF16)
    owners = [
        pl.ds(pl.multiple_of((me ^ offset) * own_rows, own_rows), own_rows)
        for offset in exchange_order(req_count)
    ]
    first = jnp.concatenate([bounds[0, owner][:, :1] for owner in owners], axis=0) - me * rows
    last = jnp.concatenate([bounds[1, owner][:, :1] for owner in owners], axis=0) - me * rows
    queries = (dot(normed, wq[...]) * HEAD_DIM ** (-0.5)).astype(BF16)

    lane_max = [jnp.full((requests, 128), NONE, F32)] * heads
    for c in range(chunks):
        keys, at = first_keys, c * CHUNK
        if at >= held:
            copies[(at - held) // CHUNK].wait()
            keys, at = last_keys, at - held
        place = c * CHUNK + lax.broadcasted_iota(jnp.int32, (requests, CHUNK), 1)
        member = (place >= first) & (place < last)
        for h in range(heads):
            cols = slice(h * HEAD_DIM, (h + 1) * HEAD_DIM)
            score = lax.dot_general(
                queries[:, cols],
                keys[at : at + CHUNK, cols],
                (((1,), (1,)), ((), ())),
                preferred_element_type=F32,
            )
            score = jnp.where(member, score, NONE)
            scores[h, :, c * CHUNK : (c + 1) * CHUNK] = score
            for t in range(CHUNK // 128):
                lane_max[h] = jnp.maximum(lane_max[h], score[:, t * 128 : (t + 1) * 128])

    peak = [jnp.max(lane_max[h], axis=1, keepdims=True) for h in range(heads)]
    mass = [jnp.zeros((requests, 128), F32)] * heads
    partial = [jnp.zeros((requests, HEAD_DIM), F32)] * heads
    for c in range(chunks):
        copies[late + c].wait()
        for h in range(heads):
            cols = slice(h * HEAD_DIM, (h + 1) * HEAD_DIM)
            expo = jnp.exp(scores[h, :, c * CHUNK : (c + 1) * CHUNK] - peak[h])
            for t in range(CHUNK // 128):
                mass[h] = mass[h] + expo[:, t * 128 : (t + 1) * 128]
            partial[h] = partial[h] + dot(
                expo.astype(BF16), values[c * CHUNK : (c + 1) * CHUNK, cols]
            )
    lane = lax.broadcasted_iota(jnp.int32, (requests, STATS), 1)
    stats = jnp.zeros((requests, STATS), F32)
    for h in range(heads):
        both = (peak[h], jnp.sum(mass[h], axis=1, keepdims=True))
        for kind, number in enumerate(both):
            for k, piece in enumerate(split_three(number)):
                stats = jnp.where(lane == (kind * heads + h) * 3 + k, piece, stats)
    for c, ref in enumerate(send_refs):
        for k, block in enumerate((c, groups + c)):
            r = slice(block * own_rows, (block + 1) * own_rows)
            for h in range(heads):
                ref[k, :, h * HEAD_DIM : (h + 1) * HEAD_DIM] = partial[h][r].astype(BF16)
            ref[k, :, head_width : head_width + STATS] = stats[r].astype(BF16)
    own_normed_ref[...] = normed[: 2 * own_rows]
    own_queries_ref[...] = queries[: 2 * own_rows].astype(F32)


def attend(tokens, gain, bounds, wq, first_keys, keys, values):
    req_count = lax.axis_size("req")
    own_rows, width = tokens[0].shape[1:]
    requests = own_rows * req_count
    rows, head_width = keys.shape
    heads = head_width // HEAD_DIM
    groups = req_count // 2
    scratch = heads * requests * rows * 4 + 4 * rows * head_width
    *sends, own_normed, own_queries = pl.pallas_call(
        functools.partial(attention_kernel, req_count, len(tokens)),
        out_shape=[jax.ShapeDtypeStruct((2, own_rows, head_width + STATS), BF16)] * groups
        + [
            jax.ShapeDtypeStruct((2 * own_rows, width), BF16),
            jax.ShapeDtypeStruct((2 * own_rows, head_width), F32),
        ],
        in_specs=[VMEM] * (len(tokens) + 4) + [ANY] * 2,
        out_specs=[VMEM] * (groups + 2),
        scratch_shapes=[
            pltpu.VMEM((rows - first_keys.shape[0], head_width), BF16),
            pltpu.VMEM((rows, head_width), BF16),
            pltpu.VMEM((heads, requests, rows), F32),
            pltpu.SemaphoreType.DMA((2 * rows // CHUNK,)),
        ],
        compiler_params=pltpu.CompilerParams(vmem_limit_bytes=scratch + LIMIT * MIB),
        name="attention",
    )(
        *tokens,
        gain,
        bounds,
        wq,
        first_keys,
        pltpu.with_memory_space_constraint(keys, pltpu.HBM),
        pltpu.with_memory_space_constraint(values, pltpu.HBM),
    )
    return sends, own_normed, own_queries


def own_kernel(normed_ref, queries_ref, wk, wv, group_ref, new_keys_ref, new_values_ref, self_ref, near_ref):
    own_rows, head_width = new_keys_ref.shape
    new_keys = dot(normed_ref[...], wk[...])[:own_rows].astype(BF16)
    new_values = dot(normed_ref[...], wv[...])[:own_rows].astype(BF16)
    new_keys_ref[...] = new_keys
    new_values_ref[...] = new_values
    product = queries_ref[:own_rows] * new_keys.astype(F32)
    lane = lax.broadcasted_iota(jnp.int32, (own_rows, STATS), 1)
    self_score = jnp.zeros((own_rows, STATS), F32)
    for h in range(head_width // HEAD_DIM):
        one = jnp.sum(product[:, h * HEAD_DIM : (h + 1) * HEAD_DIM], axis=1, keepdims=True)
        self_score = jnp.where(lane == h, one, self_score)
    self_ref[:, :head_width] = new_values.astype(F32)
    self_ref[:, head_width:] = self_score
    near_ref[...] = group_ref[1]


def own_part(normed, queries, wk, wv, group):
    own_rows, head_width = normed.shape[0] // 2, wk.shape[1]
    return pl.pallas_call(
        own_kernel,
        out_shape=[
            jax.ShapeDtypeStruct((own_rows, head_width), BF16),
            jax.ShapeDtypeStruct((own_rows, head_width), BF16),
            jax.ShapeDtypeStruct((own_rows, head_width + STATS), F32),
            jax.ShapeDtypeStruct(group.shape[1:], BF16),
        ],
        in_specs=[VMEM] * 5,
        out_specs=[VMEM] * 4,
        compiler_params=pltpu.CompilerParams(vmem_limit_bytes=LIMIT * MIB),
        name="own",
    )(normed, queries, wk, wv, group)


def merge_kernel(places, n_landed, *refs):
    landed, (self_ref, wo_ref, part_ref, sent_ref) = refs[:n_landed], refs[n_landed:]
    head_width = wo_ref.shape[0]
    heads = head_width // HEAD_DIM
    attended = []
    for h in range(heads):
        cols = slice(h * HEAD_DIM, (h + 1) * HEAD_DIM)
        self_score = self_ref[:, head_width + h : head_width + h + 1]

        def stat(a, k, kind):
            at = head_width + (kind * heads + h) * 3
            hi, mid, lo = (
                landed[a][k, :, at + j : at + j + 1].astype(F32) for j in range(3)
            )
            return hi + mid + lo

        peaks = [stat(a, k, 0) for a, k in places]
        top = functools.reduce(jnp.maximum, peaks, self_score)
        total = jnp.exp(self_score - top)
        summed = total * self_ref[:, cols]
        for (a, k), peak in zip(places, peaks):
            scale = jnp.exp(peak - top)
            total = total + scale * stat(a, k, 1)
            summed = summed + scale * landed[a][k, :, cols].astype(F32)
        attended.append((summed / total).astype(BF16))
    part = dot(jnp.concatenate(attended, axis=1), wo_ref[...])
    part_ref[...] = part
    sent_ref[...] = part.astype(BF16)


def merge(landed, self_part, wo):
    shape = (self_part.shape[0], wo.shape[1])
    return pl.pallas_call(
        functools.partial(merge_kernel, landed_blocks(lax.axis_size("req")), len(landed)),
        out_shape=(jax.ShapeDtypeStruct(shape, F32), jax.ShapeDtypeStruct(shape, BF16)),
        in_specs=[VMEM] * (len(landed) + 2),
        out_specs=(VMEM,) * 2,
        compiler_params=pltpu.CompilerParams(vmem_limit_bytes=16 * MIB),
        name="merge",
    )(*landed, self_part, wo)


def middle_kernel(*refs):
    part_ref, *others, tokens_ref, gain_ref, normed_ref, columns_ref, mid = refs
    column_width = columns_ref.shape[1]
    total = part_ref[...]
    for other in others:
        total = total + other[...].astype(F32)
    middle = tokens_ref[...].astype(F32) + total
    mid[...] = middle
    normed_ref[...] = layer_norm(middle, gain_ref[...]).astype(BF16)
    offset = pl.multiple_of(lax.axis_index("tp") * column_width, column_width)
    columns_ref[...] = mid[:, pl.ds(offset, column_width)]


def middle(part, others, tokens, gain):
    own_rows, width = tokens.shape
    return pl.pallas_call(
        middle_kernel,
        out_shape=(
            jax.ShapeDtypeStruct((own_rows, width), BF16),
            jax.ShapeDtypeStruct((own_rows, width // (1 + len(others))), F32),
        ),
        in_specs=[VMEM] * (3 + len(others)),
        out_specs=(VMEM,) * 2,
        scratch_shapes=[pltpu.VMEM((own_rows, width), F32)],
        compiler_params=pltpu.CompilerParams(vmem_limit_bytes=16 * MIB),
        name="middle",
    )(part, *others, tokens, gain)


def mlp_kernel(req_count, tp_count, n_normed, *refs):
    normed_refs, (up_ref, down_ref, up_peer_ref, down_peer_ref, out_ref) = refs[:n_normed], refs[n_normed:]
    own_rows, column_width = out_ref.shape[1:]
    me = lax.axis_index("req")
    normed = stacked(normed_refs).astype(BF16)
    activations = []
    for ref in (up_ref, up_peer_ref):
        up = dot(normed, ref[...])
        activations.append((0.5 * up * (1.0 + lax.erf(up * 0.5**0.5))).astype(BF16))
    for t in range(tp_count):
        cols = slice(t * column_width, (t + 1) * column_width)
        term = dot(activations[0], down_ref[:, cols]) + dot(activations[1], down_peer_ref[:, cols])
        for c, offset in enumerate([0] + far_offsets(req_count)):
            out_ref[((me ^ offset) // 2) * tp_count + t] = term[
                c * own_rows : (c + 1) * own_rows
            ].astype(BF16)


def mlp(normed, *weights):
    req_count, tp_count = lax.axis_size("req"), lax.axis_size("tp")
    own_rows, width = normed[0].shape[1:]
    return pl.pallas_call(
        functools.partial(mlp_kernel, req_count, tp_count, len(normed)),
        out_shape=jax.ShapeDtypeStruct(
            (req_count * tp_count // 2, own_rows, width // tp_count), BF16
        ),
        in_specs=[VMEM] * (len(normed) + len(weights)),
        out_specs=VMEM,
        compiler_params=pltpu.CompilerParams(vmem_limit_bytes=16 * MIB),
        name="mlp",
    )(*normed, *weights)


def finish_kernel(recv_ref, columns_ref, out_ref):
    total = recv_ref[0].astype(F32)
    for k in range(1, recv_ref.shape[0]):
        total = total + recv_ref[k].astype(F32)
    out_ref[...] = (columns_ref[...] + total).astype(BF16)


def finish(recv, columns):
    return pl.pallas_call(
        finish_kernel,
        out_shape=jax.ShapeDtypeStruct(columns.shape, BF16),
        in_specs=[VMEM] * 2,
        out_specs=VMEM,
        compiler_params=pltpu.CompilerParams(vmem_limit_bytes=16 * MIB),
        name="finish",
    )(recv, columns)


def body(
    tokens,
    first_gain,
    query_weight,
    key_weight,
    value_weight,
    out_weight,
    second_gain,
    up_weight,
    down_weight,
    cache_keys,
    cache_values,
    lengths,
    stream_order,
):
    req_count = lax.axis_size("req")
    tp_count = lax.axis_size("tp")
    up_peer, down_peer = swap(up_weight, "req", 1), swap(down_weight, "req", 1)
    far = gather_far(tokens)
    tokens, gain, wq, first_keys, bounds = load(
        lengths[None],
        stream_order[None],
        tokens,
        first_gain[None],
        query_weight,
        cache_keys,
        last_rows=cache_keys.shape[0] // 2,
    )
    sends, own_normed, own_queries = attend(
        gather_near(tokens, far), gain, bounds, wq, first_keys, cache_keys, cache_values
    )
    new_keys, new_values, self_part, near = own_part(
        own_normed, own_queries, key_weight, value_weight, sends[0]
    )
    landed = scatter_far(sends)
    landed.append(scatter_near(near, landed[1:]))
    part, sent = merge(landed, self_part, out_weight)
    others = [swap(sent, "tp", m) for m in range(1, tp_count)]
    normed, columns = middle(part, others, tokens, second_gain[None])
    all_normed = [part[None] for part in [normed] + gather_far(normed)]
    term = mlp(all_normed, up_weight, down_weight, up_peer, down_peer)
    same_core = [
        [i * tp_count + t for i in range(core, req_count, 2) for t in range(tp_count)]
        for core in range(2)
    ]
    terms = lax.all_to_all(
        term,
        ("req", "tp"),
        split_axis=0,
        concat_axis=0,
        tiled=True,
        axis_index_groups=same_core,
    )
    hidden = finish(terms, columns)
    return (hidden, new_keys, new_values)


def solution(mesh):
    return jax.shard_map(
        body,
        mesh=mesh,
        in_specs=(
            P("req", None),
            P(),
            P(None, "tp"),
            P(None, "tp"),
            P(None, "tp"),
            P("tp", None),
            P(),
            P(None, ("req", "tp")),
            P(("req", "tp"), None),
            P("req", "tp"),
            P("req", "tp"),
            P(),
            P(),
        ),
        out_specs=(P("req", "tp"), P("req", "tp"), P("req", "tp")),
        check_vma=False,
    )
```

```python
import functools

import jax
import jax.numpy as jnp
from jax import lax
from jax.experimental import pallas as pl
from jax.experimental.pallas import tpu as pltpu
from jax.sharding import PartitionSpec as P

HEAD_DIM = 128
STATS = 128
NONE = -1e30
CHUNK = 1024
MIB = 1 << 20
LIMIT = 8
VMEM = pl.BlockSpec(memory_space=pltpu.VMEM)
ANY = pl.BlockSpec(memory_space=pl.ANY)
F32 = jnp.float32
BF16 = jnp.bfloat16


def layer_norm(values, gain_vector):
    center = jnp.mean(values, axis=-1, keepdims=True)
    shifted = values - center
    spread = jnp.mean(shifted * shifted, axis=-1, keepdims=True)
    return shifted * lax.rsqrt(spread + 1e-05) * gain_vector


def dot(a, b):
    return jnp.dot(a, b, preferred_element_type=F32)


def stream_ranges(lens_row, order_row):
    n = lens_row.shape[1]
    down = lax.broadcasted_iota(jnp.int32, (n, n), 0)
    across = lax.broadcasted_iota(jnp.int32, (n, n), 1)
    lens = lens_row.astype(F32)
    eye = down == across
    lens_col = jnp.sum(jnp.where(eye, lens, 0.0), axis=1, keepdims=True)
    holds = order_row == down
    slot_len = jnp.sum(jnp.where(holds, lens_col, 0.0), axis=0, keepdims=True)
    slot_len_col = jnp.sum(jnp.where(eye, slot_len, 0.0), axis=1, keepdims=True)
    before = jnp.sum(jnp.where(down < across, slot_len_col, 0.0), axis=0, keepdims=True)
    first = jnp.sum(jnp.where(holds, before, 0.0), axis=1, keepdims=True)
    return first.astype(jnp.int32), (first + lens_col).astype(jnp.int32)


TERM_ORDER = (14, 12, 4, 5, 15, 8, 11, 10, 1, 7, 6, 13, 3, 0, 9, 2)


def term_order(req_count, tp_count):
    n = req_count * tp_count // 2
    return TERM_ORDER if n == len(TERM_ORDER) else tuple(range(n))


def swap(x, axis, offset):
    n = lax.axis_size(axis)
    return lax.ppermute(x, axis, [(i, i ^ offset) for i in range(n)])


def far_offsets(n):
    return list(range(n - 2, 0, -2))


def exchange_order(n):
    same = [0] + far_offsets(n)
    return same + [offset + 1 for offset in same]


def gather_far(x):
    return [swap(x, "req", m) for m in far_offsets(lax.axis_size("req"))]


def gather_near(x, far):
    return [x[None]] + [part[None] for part in far] + [swap(jnp.stack([x] + far), "req", 1)]


def scatter_far(groups):
    offsets = far_offsets(lax.axis_size("req"))
    return groups[:1] + [swap(group, "req", m) for group, m in zip(groups[1:], offsets)]


def scatter_near(near, far):
    return swap(jnp.stack([near] + [part[1] for part in far]), "req", 1)


def landed_blocks(n):
    return [(c, 0) for c in range(n // 2)] + [(n // 2, c) for c in range(n // 2)]


def split_three(x):
    parts = []
    for _ in range(3):
        parts.append(x.astype(BF16).astype(F32))
        x = x - parts[-1]
    return parts


def stacked(refs):
    blocks = [ref[k].astype(F32) for ref in refs for k in range(ref.shape[0])]
    return jnp.concatenate(blocks, axis=0)


def load_kernel(n, *refs):
    sources, targets = refs[:n], refs[n : 2 * n - 2]
    bounds_ref, lens, order, sems = refs[2 * n - 2 :]
    targets = (lens, order) + targets
    copies = [
        pltpu.make_async_copy(source.at[pl.ds(0, target.shape[0])], target, sems.at[k])
        for k, (source, target) in enumerate(zip(sources, targets))
    ]
    for copy in copies:
        copy.start()
    copies[0].wait()
    copies[1].wait()
    first, last = stream_ranges(lens[...], order[...])
    bounds_ref[0] = jnp.broadcast_to(first, bounds_ref.shape[1:])
    bounds_ref[1] = jnp.broadcast_to(last, bounds_ref.shape[1:])
    for copy in copies[2:]:
        copy.wait()


def load(lens, order, *arrays, last_rows):
    sources = [pltpu.with_memory_space_constraint(x, pltpu.HBM) for x in (lens, order) + arrays]
    last = arrays[-1]
    return pl.pallas_call(
        functools.partial(load_kernel, len(sources)),
        out_shape=[pltpu.VMEM(x.shape, x.dtype) for x in arrays[:-1]]
        + [pltpu.VMEM((last_rows, last.shape[1]), last.dtype)]
        + [pltpu.VMEM((2, lens.shape[1], 128), jnp.int32)],
        in_specs=[ANY] * len(sources),
        out_specs=[VMEM] * (len(arrays) + 1),
        scratch_shapes=[
            pltpu.VMEM(lens.shape, jnp.int32),
            pltpu.VMEM(order.shape, jnp.int32),
            pltpu.SemaphoreType.DMA((len(sources),)),
        ],
        compiler_params=pltpu.CompilerParams(vmem_limit_bytes=LIMIT * MIB),
        cost_estimate=pl.CostEstimate(
            flops=0, bytes_accessed=2 * sum(x.size for x in arrays), transcendentals=0
        ),
        name="load",
    )(*sources)


def attention_kernel(req_count, n_tokens, *refs):
    token_refs, refs = refs[:n_tokens], refs[n_tokens:]
    gain_ref, bounds, wq, first_keys, keys_hbm, values_hbm = refs[:6]
    groups = req_count // 2
    send_refs, refs = refs[6 : 6 + groups], refs[6 + groups :]
    own_normed_ref, own_queries_ref, last_keys, values, scores, sems = refs
    rows, head_width = values.shape
    held = first_keys.shape[0]
    heads = head_width // HEAD_DIM
    chunks = rows // CHUNK
    own_rows = own_normed_ref.shape[0] // 2
    requests = own_rows * req_count
    me = lax.axis_index("req")

    copies = []
    for c in range(held // CHUNK, chunks):
        there, here = pl.ds(c * CHUNK, CHUNK), pl.ds(c * CHUNK - held, CHUNK)
        copies.append(
            pltpu.make_async_copy(keys_hbm.at[there], last_keys.at[here], sems.at[len(copies)])
        )
    late = len(copies)
    for c in range(chunks):
        part = pl.ds(c * CHUNK, CHUNK)
        copies.append(
            pltpu.make_async_copy(values_hbm.at[part], values.at[part], sems.at[len(copies)])
        )
    for copy in copies:
        copy.start()
    normed = layer_norm(stacked(token_refs), gain_ref[...]).astype(BF16)
    owners = [
        pl.ds(pl.multiple_of((me ^ offset) * own_rows, own_rows), own_rows)
        for offset in exchange_order(req_count)
    ]
    first = jnp.concatenate([bounds[0, owner][:, :1] for owner in owners], axis=0) - me * rows
    last = jnp.concatenate([bounds[1, owner][:, :1] for owner in owners], axis=0) - me * rows
    queries = (dot(normed, wq[...]) * HEAD_DIM ** (-0.5)).astype(BF16)

    pairs = heads // 2
    two = 2 * requests
    wide = 2 * HEAD_DIM
    zero = jnp.zeros((requests, HEAD_DIM), BF16)
    paired = []
    for p in range(pairs):
        left = queries[:, p * wide : p * wide + HEAD_DIM]
        right = queries[:, p * wide + HEAD_DIM : (p + 1) * wide]
        upper = jnp.concatenate([left, zero], axis=1)
        lower = jnp.concatenate([zero, right], axis=1)
        paired.append(jnp.concatenate([upper, lower], axis=0))
    lane_max = [jnp.full((two, 128), NONE, F32)] * pairs
    for c in range(chunks):
        keys, at = first_keys, c * CHUNK
        if at >= held:
            copies[(at - held) // CHUNK].wait()
            keys, at = last_keys, at - held
        place = c * CHUNK + lax.broadcasted_iota(jnp.int32, (requests, CHUNK), 1)
        member = (place >= first) & (place < last)
        for p in range(pairs):
            score = lax.dot_general(
                paired[p],
                keys[at : at + CHUNK, p * wide : (p + 1) * wide],
                (((1,), (1,)), ((), ())),
                preferred_element_type=F32,
            )
            score = jnp.concatenate(
                [
                    jnp.where(member, score[:requests], NONE),
                    jnp.where(member, score[requests:], NONE),
                ],
                axis=0,
            )
            scores[p, :, c * CHUNK : (c + 1) * CHUNK] = score
            for t in range(CHUNK // 128):
                lane_max[p] = jnp.maximum(lane_max[p], score[:, t * 128 : (t + 1) * 128])

    tops = [jnp.max(lane_max[p], axis=1, keepdims=True) for p in range(pairs)]
    sums = [jnp.zeros((two, 128), F32)] * pairs
    outs = [jnp.zeros((two, wide), F32)] * pairs
    for c in range(chunks):
        copies[late + c].wait()
        for p in range(pairs):
            expo = jnp.exp(scores[p, :, c * CHUNK : (c + 1) * CHUNK] - tops[p])
            for t in range(CHUNK // 128):
                sums[p] = sums[p] + expo[:, t * 128 : (t + 1) * 128]
            outs[p] = outs[p] + dot(
                expo.astype(BF16),
                values[c * CHUNK : (c + 1) * CHUNK, p * wide : (p + 1) * wide],
            )
    peak, mass, partial = [], [], []
    for h in range(heads):
        p, r = h // 2, slice(h % 2 * requests, (h % 2 + 1) * requests)
        peak.append(tops[p][r])
        mass.append(sums[p][r])
        partial.append(outs[p][r, h % 2 * HEAD_DIM : (h % 2 + 1) * HEAD_DIM])
    lane = lax.broadcasted_iota(jnp.int32, (requests, STATS), 1)
    stats = jnp.zeros((requests, STATS), F32)
    for h in range(heads):
        both = (peak[h], jnp.sum(mass[h], axis=1, keepdims=True))
        for kind, number in enumerate(both):
            for k, piece in enumerate(split_three(number)):
                stats = jnp.where(lane == (k * 2 + kind) * heads + h, piece, stats)
    for c, ref in enumerate(send_refs):
        for k, block in enumerate((c, groups + c)):
            r = slice(block * own_rows, (block + 1) * own_rows)
            for h in range(heads):
                ref[k, :, h * HEAD_DIM : (h + 1) * HEAD_DIM] = partial[h][r].astype(BF16)
            ref[k, :, head_width : head_width + STATS] = stats[r].astype(BF16)
    own_normed_ref[...] = normed[: 2 * own_rows]
    own_queries_ref[...] = queries[: 2 * own_rows].astype(F32)


def attend(tokens, gain, bounds, wq, first_keys, keys, values):
    req_count = lax.axis_size("req")
    own_rows, width = tokens[0].shape[1:]
    requests = own_rows * req_count
    rows, head_width = keys.shape
    heads = head_width // HEAD_DIM
    groups = req_count // 2
    scratch = heads * requests * rows * 4 + 4 * rows * head_width
    *sends, own_normed, own_queries = pl.pallas_call(
        functools.partial(attention_kernel, req_count, len(tokens)),
        out_shape=[jax.ShapeDtypeStruct((2, own_rows, head_width + STATS), BF16)] * groups
        + [
            jax.ShapeDtypeStruct((2 * own_rows, width), BF16),
            jax.ShapeDtypeStruct((2 * own_rows, head_width), F32),
        ],
        in_specs=[VMEM] * (len(tokens) + 4) + [ANY] * 2,
        out_specs=[VMEM] * (groups + 2),
        scratch_shapes=[
            pltpu.VMEM((rows - first_keys.shape[0], head_width), BF16),
            pltpu.VMEM((rows, head_width), BF16),
            pltpu.VMEM((heads // 2, 2 * requests, rows), F32),
            pltpu.SemaphoreType.DMA((2 * rows // CHUNK,)),
        ],
        compiler_params=pltpu.CompilerParams(vmem_limit_bytes=scratch + LIMIT * MIB),
        name="attention",
    )(
        *tokens,
        gain,
        bounds,
        wq,
        first_keys,
        pltpu.with_memory_space_constraint(keys, pltpu.HBM),
        pltpu.with_memory_space_constraint(values, pltpu.HBM),
    )
    return sends, own_normed, own_queries


def own_kernel(normed_ref, queries_ref, wk, wv, group_ref, new_keys_ref, new_values_ref, self_ref, near_ref):
    own_rows, head_width = new_keys_ref.shape
    new_keys = dot(normed_ref[...], wk[...])[:own_rows].astype(BF16)
    new_values = dot(normed_ref[...], wv[...])[:own_rows].astype(BF16)
    new_keys_ref[...] = new_keys
    new_values_ref[...] = new_values
    product = queries_ref[:own_rows] * new_keys.astype(F32)
    lane = lax.broadcasted_iota(jnp.int32, (own_rows, STATS), 1)
    self_score = jnp.zeros((own_rows, STATS), F32)
    for h in range(head_width // HEAD_DIM):
        one = jnp.sum(product[:, h * HEAD_DIM : (h + 1) * HEAD_DIM], axis=1, keepdims=True)
        self_score = jnp.where(lane == h, one, self_score)
    self_ref[:, :head_width] = new_values.astype(F32)
    self_ref[:, head_width:] = self_score
    near_ref[...] = group_ref[1]


def own_part(normed, queries, wk, wv, group):
    own_rows, head_width = normed.shape[0] // 2, wk.shape[1]
    return pl.pallas_call(
        own_kernel,
        out_shape=[
            jax.ShapeDtypeStruct((own_rows, head_width), BF16),
            jax.ShapeDtypeStruct((own_rows, head_width), BF16),
            jax.ShapeDtypeStruct((own_rows, head_width + STATS), F32),
            jax.ShapeDtypeStruct(group.shape[1:], BF16),
        ],
        in_specs=[VMEM] * 5,
        out_specs=[VMEM] * 4,
        compiler_params=pltpu.CompilerParams(vmem_limit_bytes=LIMIT * MIB),
        name="own",
    )(normed, queries, wk, wv, group)


def merge_kernel(places, n_landed, *refs):
    landed, (self_ref, wo_ref, part_ref, sent_ref) = refs[:n_landed], refs[n_landed:]
    head_width = wo_ref.shape[0]
    heads = head_width // HEAD_DIM
    self_scores = self_ref[:, head_width:]

    def left(x, n):
        return pltpu.roll(x, STATS - n, 1)

    stats = []
    for a, k in places:
        pieces = landed[a][k, :, head_width:].astype(F32)
        stats.append(pieces + left(pieces, 2 * heads) + left(pieces, 4 * heads))
    top = functools.reduce(jnp.maximum, stats, self_scores)
    self_weight = jnp.exp(self_scores - top)
    scales = [jnp.exp(stat - top) for stat in stats]
    total = self_weight
    for stat, scale in zip(stats, scales):
        total = total + scale * left(stat, heads)
    attended = []
    for h in range(heads):
        cols = slice(h * HEAD_DIM, (h + 1) * HEAD_DIM)
        summed = self_weight[:, h : h + 1] * self_ref[:, cols]
        for (a, k), scale in zip(places, scales):
            summed = summed + scale[:, h : h + 1] * landed[a][k, :, cols].astype(F32)
        attended.append((summed / total[:, h : h + 1]).astype(BF16))
    part = dot(jnp.concatenate(attended, axis=1), wo_ref[...])
    part_ref[...] = part
    sent_ref[...] = part.astype(BF16)


def merge(landed, self_part, wo):
    shape = (self_part.shape[0], wo.shape[1])
    return pl.pallas_call(
        functools.partial(merge_kernel, landed_blocks(lax.axis_size("req")), len(landed)),
        out_shape=(jax.ShapeDtypeStruct(shape, F32), jax.ShapeDtypeStruct(shape, BF16)),
        in_specs=[VMEM] * (len(landed) + 2),
        out_specs=(VMEM,) * 2,
        compiler_params=pltpu.CompilerParams(vmem_limit_bytes=16 * MIB),
        name="merge",
    )(*landed, self_part, wo)


def middle_kernel(*refs):
    part_ref, *others, tokens_ref, gain_ref, normed_ref, columns_ref, mid = refs
    column_width = columns_ref.shape[1]
    total = part_ref[...]
    for other in others:
        total = total + other[...].astype(F32)
    middle = tokens_ref[...].astype(F32) + total
    mid[...] = middle
    normed_ref[...] = layer_norm(middle, gain_ref[...]).astype(BF16)
    offset = pl.multiple_of(lax.axis_index("tp") * column_width, column_width)
    columns_ref[...] = mid[:, pl.ds(offset, column_width)]


def middle(part, others, tokens, gain):
    own_rows, width = tokens.shape
    return pl.pallas_call(
        middle_kernel,
        out_shape=(
            jax.ShapeDtypeStruct((own_rows, width), BF16),
            jax.ShapeDtypeStruct((own_rows, width // (1 + len(others))), F32),
        ),
        in_specs=[VMEM] * (3 + len(others)),
        out_specs=(VMEM,) * 2,
        scratch_shapes=[pltpu.VMEM((own_rows, width), F32)],
        compiler_params=pltpu.CompilerParams(vmem_limit_bytes=16 * MIB),
        name="middle",
    )(part, *others, tokens, gain)


def mlp_kernel(req_count, tp_count, n_normed, *refs):
    normed_refs, (up_ref, down_ref, up_peer_ref, down_peer_ref, out_ref) = refs[:n_normed], refs[n_normed:]
    own_rows, column_width = out_ref.shape[1:]
    me = lax.axis_index("req")
    normed = stacked(normed_refs).astype(BF16)
    order = term_order(req_count, tp_count)
    activations = []
    for ref in (up_ref, up_peer_ref):
        up = dot(normed, ref[...])
        activations.append((0.5 * up * (1.0 + lax.erf(up * 0.5**0.5))).astype(BF16))
    for t in range(tp_count):
        cols = slice(t * column_width, (t + 1) * column_width)
        term = dot(activations[0], down_ref[:, cols]) + dot(activations[1], down_peer_ref[:, cols])
        for c, offset in enumerate([0] + far_offsets(req_count)):
            chip, place = (me ^ offset) // 2, 0
            for other in range(req_count // 2):
                place = jnp.where(chip == other, order.index(other * tp_count + t), place)
            out_ref[place] = term[c * own_rows : (c + 1) * own_rows].astype(BF16)


def mlp(normed, *weights):
    req_count, tp_count = lax.axis_size("req"), lax.axis_size("tp")
    own_rows, width = normed[0].shape[1:]
    return pl.pallas_call(
        functools.partial(mlp_kernel, req_count, tp_count, len(normed)),
        out_shape=jax.ShapeDtypeStruct(
            (req_count * tp_count // 2, own_rows, width // tp_count), BF16
        ),
        in_specs=[VMEM] * (len(normed) + len(weights)),
        out_specs=VMEM,
        compiler_params=pltpu.CompilerParams(vmem_limit_bytes=16 * MIB),
        name="mlp",
    )(*normed, *weights)


def finish_kernel(recv_ref, columns_ref, out_ref):
    total = recv_ref[0].astype(F32)
    for k in range(1, recv_ref.shape[0]):
        total = total + recv_ref[k].astype(F32)
    out_ref[...] = (columns_ref[...] + total).astype(BF16)


def finish(recv, columns):
    return pl.pallas_call(
        finish_kernel,
        out_shape=jax.ShapeDtypeStruct(columns.shape, BF16),
        in_specs=[VMEM] * 2,
        out_specs=VMEM,
        compiler_params=pltpu.CompilerParams(vmem_limit_bytes=16 * MIB),
        name="finish",
    )(recv, columns)


def body(
    tokens,
    first_gain,
    query_weight,
    key_weight,
    value_weight,
    out_weight,
    second_gain,
    up_weight,
    down_weight,
    cache_keys,
    cache_values,
    lengths,
    stream_order,
):
    req_count = lax.axis_size("req")
    tp_count = lax.axis_size("tp")
    up_peer, down_peer = swap(up_weight, "req", 1), swap(down_weight, "req", 1)
    far = gather_far(tokens)
    tokens, gain, wq, first_keys, bounds = load(
        lengths[None],
        stream_order[None],
        tokens,
        first_gain[None],
        query_weight,
        cache_keys,
        last_rows=cache_keys.shape[0] * 3 // 4,
    )
    sends, own_normed, own_queries = attend(
        gather_near(tokens, far), gain, bounds, wq, first_keys, cache_keys, cache_values
    )
    new_keys, new_values, self_part, near = own_part(
        own_normed, own_queries, key_weight, value_weight, sends[0]
    )
    landed = scatter_far(sends)
    landed.append(scatter_near(near, landed[1:]))
    part, sent = merge(landed, self_part, out_weight)
    others = [swap(sent, "tp", m) for m in range(1, tp_count)]
    normed, columns = middle(part, others, tokens, second_gain[None])
    all_normed = [part[None] for part in [normed] + gather_far(normed)]
    term = mlp(all_normed, up_weight, down_weight, up_peer, down_peer)
    order = term_order(req_count, tp_count)
    same_core = [
        [(2 * (k // tp_count) + core) * tp_count + k % tp_count for k in order]
        for core in range(2)
    ]
    terms = lax.all_to_all(
        term,
        ("req", "tp"),
        split_axis=0,
        concat_axis=0,
        tiled=True,
        axis_index_groups=same_core,
    )
    hidden = finish(terms, columns)
    return (hidden, new_keys, new_values)


def solution(mesh):
    return jax.shard_map(
        body,
        mesh=mesh,
        in_specs=(
            P("req", None),
            P(),
            P(None, "tp"),
            P(None, "tp"),
            P(None, "tp"),
            P("tp", None),
            P(),
            P(None, ("req", "tp")),
            P(("req", "tp"), None),
            P("req", "tp"),
            P("req", "tp"),
            P(),
            P(),
        ),
        out_specs=(P("req", "tp"), P("req", "tp"), P("req", "tp")),
        check_vma=False,
    )
```

```python
import functools

import jax
import jax.numpy as jnp
from jax import lax
from jax.experimental import pallas as pl
from jax.experimental.pallas import tpu as pltpu
from jax.sharding import PartitionSpec as P

HEAD_DIM = 128
STATS = 128
NONE = -1e30
CHUNK = 1024
MIB = 1 << 20
LIMIT = 8
VMEM = pl.BlockSpec(memory_space=pltpu.VMEM)
ANY = pl.BlockSpec(memory_space=pl.ANY)
F32 = jnp.float32
BF16 = jnp.bfloat16


def layer_norm(values, gain_vector):
    center = jnp.mean(values, axis=-1, keepdims=True)
    shifted = values - center
    spread = jnp.mean(shifted * shifted, axis=-1, keepdims=True)
    return shifted * lax.rsqrt(spread + 1e-05) * gain_vector


def dot(a, b):
    return jnp.dot(a, b, preferred_element_type=F32)


def stream_ranges(lens_row, order_row):
    n = lens_row.shape[1]
    down = lax.broadcasted_iota(jnp.int32, (n, n), 0)
    across = lax.broadcasted_iota(jnp.int32, (n, n), 1)
    lens = lens_row.astype(F32)
    eye = down == across
    lens_col = jnp.sum(jnp.where(eye, lens, 0.0), axis=1, keepdims=True)
    holds = order_row == down
    slot_len = jnp.sum(jnp.where(holds, lens_col, 0.0), axis=0, keepdims=True)
    slot_len_col = jnp.sum(jnp.where(eye, slot_len, 0.0), axis=1, keepdims=True)
    before = jnp.sum(jnp.where(down < across, slot_len_col, 0.0), axis=0, keepdims=True)
    first = jnp.sum(jnp.where(holds, before, 0.0), axis=1, keepdims=True)
    return first.astype(jnp.int32), (first + lens_col).astype(jnp.int32)


TERM_ORDER = (14, 12, 4, 5, 15, 8, 11, 10, 1, 7, 6, 13, 3, 0, 9, 2)


def term_order(req_count, tp_count):
    n = req_count * tp_count // 2
    return TERM_ORDER if n == len(TERM_ORDER) else tuple(range(n))


def swap(x, axis, offset):
    n = lax.axis_size(axis)
    return lax.ppermute(x, axis, [(i, i ^ offset) for i in range(n)])


def far_offsets(n):
    return list(range(n - 2, 0, -2))


def exchange_order(n):
    same = [0] + far_offsets(n)
    return same + [offset + 1 for offset in same]


def gather_far(x):
    return [swap(x, "req", m) for m in far_offsets(lax.axis_size("req"))]


def gather_near(x, far):
    return [x[None]] + [part[None] for part in far] + [swap(jnp.stack([x] + far), "req", 1)]


def scatter_far(groups):
    offsets = far_offsets(lax.axis_size("req"))
    return groups[:1] + [swap(group, "req", m) for group, m in zip(groups[1:], offsets)]


def scatter_near(near, far):
    return swap(jnp.stack([near] + [part[1] for part in far]), "req", 1)


def landed_blocks(n):
    return [(c, 0) for c in range(n // 2)] + [(n // 2, c) for c in range(n // 2)]


def split_three(x):
    parts = []
    for _ in range(3):
        parts.append(x.astype(BF16).astype(F32))
        x = x - parts[-1]
    return parts


def stacked(refs):
    blocks = [ref[k].astype(F32) for ref in refs for k in range(ref.shape[0])]
    return jnp.concatenate(blocks, axis=0)


def load_kernel(n, *refs):
    sources, targets = refs[:n], refs[n : 2 * n - 2]
    bounds_ref, lens, order, sems = refs[2 * n - 2 :]
    targets = (lens, order) + targets
    copies = [
        pltpu.make_async_copy(source.at[pl.ds(0, target.shape[0])], target, sems.at[k])
        for k, (source, target) in enumerate(zip(sources, targets))
    ]
    for copy in copies:
        copy.start()
    copies[0].wait()
    copies[1].wait()
    first, last = stream_ranges(lens[...], order[...])
    bounds_ref[0] = jnp.broadcast_to(first, bounds_ref.shape[1:])
    bounds_ref[1] = jnp.broadcast_to(last, bounds_ref.shape[1:])
    for copy in copies[2:]:
        copy.wait()


def load(lens, order, *arrays, last_rows):
    sources = [pltpu.with_memory_space_constraint(x, pltpu.HBM) for x in (lens, order) + arrays]
    last = arrays[-1]
    return pl.pallas_call(
        functools.partial(load_kernel, len(sources)),
        out_shape=[pltpu.VMEM(x.shape, x.dtype) for x in arrays[:-1]]
        + [pltpu.VMEM((last_rows, last.shape[1]), last.dtype)]
        + [pltpu.VMEM((2, lens.shape[1], 128), jnp.int32)],
        in_specs=[ANY] * len(sources),
        out_specs=[VMEM] * (len(arrays) + 1),
        scratch_shapes=[
            pltpu.VMEM(lens.shape, jnp.int32),
            pltpu.VMEM(order.shape, jnp.int32),
            pltpu.SemaphoreType.DMA((len(sources),)),
        ],
        compiler_params=pltpu.CompilerParams(vmem_limit_bytes=LIMIT * MIB),
        cost_estimate=pl.CostEstimate(
            flops=0, bytes_accessed=2 * sum(x.size for x in arrays), transcendentals=0
        ),
        name="load",
    )(*sources)


def attention_kernel(req_count, n_tokens, *refs):
    token_refs, refs = refs[:n_tokens], refs[n_tokens:]
    gain_ref, bounds, wq, first_keys, keys_hbm, values_hbm = refs[:6]
    groups = req_count // 2
    send_refs, refs = refs[6 : 6 + groups], refs[6 + groups :]
    own_normed_ref, own_queries_ref, last_keys, values, scores, sems = refs
    rows, head_width = values.shape
    held = first_keys.shape[0]
    heads = head_width // HEAD_DIM
    chunks = rows // CHUNK
    own_rows = own_normed_ref.shape[0] // 2
    requests = own_rows * req_count
    me = lax.axis_index("req")

    copies = []
    for c in range(held // CHUNK, chunks):
        there, here = pl.ds(c * CHUNK, CHUNK), pl.ds(c * CHUNK - held, CHUNK)
        copies.append(
            pltpu.make_async_copy(keys_hbm.at[there], last_keys.at[here], sems.at[len(copies)])
        )
    late = len(copies)
    for c in range(chunks):
        part = pl.ds(c * CHUNK, CHUNK)
        copies.append(
            pltpu.make_async_copy(values_hbm.at[part], values.at[part], sems.at[len(copies)])
        )
    for copy in copies:
        copy.start()
    normed = layer_norm(stacked(token_refs), gain_ref[...]).astype(BF16)
    owners = [
        pl.ds(pl.multiple_of((me ^ offset) * own_rows, own_rows), own_rows)
        for offset in exchange_order(req_count)
    ]
    first = jnp.concatenate([bounds[0, owner][:, :1] for owner in owners], axis=0) - me * rows
    last = jnp.concatenate([bounds[1, owner][:, :1] for owner in owners], axis=0) - me * rows
    queries = (dot(normed, wq[...]) * HEAD_DIM ** (-0.5)).astype(BF16)

    pairs = heads // 2
    two = 2 * requests
    wide = 2 * HEAD_DIM
    zero = jnp.zeros((requests, HEAD_DIM), BF16)
    paired = []
    for p in range(pairs):
        left = queries[:, p * wide : p * wide + HEAD_DIM]
        right = queries[:, p * wide + HEAD_DIM : (p + 1) * wide]
        upper = jnp.concatenate([left, zero], axis=1)
        lower = jnp.concatenate([zero, right], axis=1)
        paired.append(jnp.concatenate([upper, lower], axis=0))
    lane_max = [jnp.full((two, 128), NONE, F32)] * pairs
    for c in range(chunks):
        keys, at = first_keys, c * CHUNK
        if at >= held:
            copies[(at - held) // CHUNK].wait()
            keys, at = last_keys, at - held
        place = c * CHUNK + lax.broadcasted_iota(jnp.int32, (requests, CHUNK), 1)
        member = (place >= first) & (place < last)
        for p in range(pairs):
            score = lax.dot_general(
                paired[p],
                keys[at : at + CHUNK, p * wide : (p + 1) * wide],
                (((1,), (1,)), ((), ())),
                preferred_element_type=F32,
            )
            score = jnp.concatenate(
                [
                    jnp.where(member, score[:requests], NONE),
                    jnp.where(member, score[requests:], NONE),
                ],
                axis=0,
            )
            scores[p, :, c * CHUNK : (c + 1) * CHUNK] = score
            for t in range(CHUNK // 128):
                lane_max[p] = jnp.maximum(lane_max[p], score[:, t * 128 : (t + 1) * 128])

    tops = [jnp.max(lane_max[p], axis=1, keepdims=True) for p in range(pairs)]
    sums = [jnp.zeros((two, 128), F32)] * pairs
    outs = [jnp.zeros((two, wide), F32)] * pairs
    for c in range(chunks):
        copies[late + c].wait()
        for p in range(pairs):
            expo = jnp.exp(scores[p, :, c * CHUNK : (c + 1) * CHUNK] - tops[p])
            for t in range(CHUNK // 128):
                sums[p] = sums[p] + expo[:, t * 128 : (t + 1) * 128]
            outs[p] = outs[p] + dot(
                expo.astype(BF16),
                values[c * CHUNK : (c + 1) * CHUNK, p * wide : (p + 1) * wide],
            )
    peak, mass, partial = [], [], []
    for h in range(heads):
        p, r = h // 2, slice(h % 2 * requests, (h % 2 + 1) * requests)
        peak.append(tops[p][r])
        mass.append(sums[p][r])
        partial.append(outs[p][r, h % 2 * HEAD_DIM : (h % 2 + 1) * HEAD_DIM])
    lane = lax.broadcasted_iota(jnp.int32, (requests, STATS), 1)
    stats = jnp.zeros((requests, STATS), F32)
    for h in range(heads):
        both = (peak[h], jnp.sum(mass[h], axis=1, keepdims=True))
        for kind, number in enumerate(both):
            for k, piece in enumerate(split_three(number)):
                stats = jnp.where(lane == (k * 2 + kind) * heads + h, piece, stats)
    for c, ref in enumerate(send_refs):
        for k, block in enumerate((c, groups + c)):
            r = slice(block * own_rows, (block + 1) * own_rows)
            for h in range(heads):
                ref[k, :, h * HEAD_DIM : (h + 1) * HEAD_DIM] = partial[h][r].astype(BF16)
            ref[k, :, head_width : head_width + STATS] = stats[r].astype(BF16)
    own_normed_ref[...] = normed[: 2 * own_rows]
    own_queries_ref[...] = queries[: 2 * own_rows].astype(F32)


def attend(tokens, gain, bounds, wq, first_keys, keys, values):
    req_count = lax.axis_size("req")
    own_rows, width = tokens[0].shape[1:]
    requests = own_rows * req_count
    rows, head_width = keys.shape
    heads = head_width // HEAD_DIM
    groups = req_count // 2
    scratch = heads * requests * rows * 4 + 4 * rows * head_width
    *sends, own_normed, own_queries = pl.pallas_call(
        functools.partial(attention_kernel, req_count, len(tokens)),
        out_shape=[jax.ShapeDtypeStruct((2, own_rows, head_width + STATS), BF16)] * groups
        + [
            jax.ShapeDtypeStruct((2 * own_rows, width), BF16),
            jax.ShapeDtypeStruct((2 * own_rows, head_width), F32),
        ],
        in_specs=[VMEM] * (len(tokens) + 4) + [ANY] * 2,
        out_specs=[VMEM] * (groups + 2),
        scratch_shapes=[
            pltpu.VMEM((rows - first_keys.shape[0], head_width), BF16),
            pltpu.VMEM((rows, head_width), BF16),
            pltpu.VMEM((heads // 2, 2 * requests, rows), F32),
            pltpu.SemaphoreType.DMA((2 * rows // CHUNK,)),
        ],
        compiler_params=pltpu.CompilerParams(vmem_limit_bytes=scratch + LIMIT * MIB),
        name="attention",
    )(
        *tokens,
        gain,
        bounds,
        wq,
        first_keys,
        pltpu.with_memory_space_constraint(keys, pltpu.HBM),
        pltpu.with_memory_space_constraint(values, pltpu.HBM),
    )
    return sends, own_normed, own_queries


def own_kernel(normed_ref, queries_ref, wk, wv, group_ref, new_keys_ref, new_values_ref, self_ref, near_ref):
    own_rows, head_width = new_keys_ref.shape
    new_keys = dot(normed_ref[...], wk[...])[:own_rows].astype(BF16)
    new_values = dot(normed_ref[...], wv[...])[:own_rows].astype(BF16)
    new_keys_ref[...] = new_keys
    new_values_ref[...] = new_values
    product = queries_ref[:own_rows] * new_keys.astype(F32)
    lane = lax.broadcasted_iota(jnp.int32, (own_rows, STATS), 1)
    self_score = jnp.zeros((own_rows, STATS), F32)
    for h in range(head_width // HEAD_DIM):
        one = jnp.sum(product[:, h * HEAD_DIM : (h + 1) * HEAD_DIM], axis=1, keepdims=True)
        self_score = jnp.where(lane == h, one, self_score)
    self_ref[:, :head_width] = new_values.astype(F32)
    self_ref[:, head_width:] = self_score
    near_ref[...] = group_ref[1]


def own_part(normed, queries, wk, wv, group):
    own_rows, head_width = normed.shape[0] // 2, wk.shape[1]
    return pl.pallas_call(
        own_kernel,
        out_shape=[
            jax.ShapeDtypeStruct((own_rows, head_width), BF16),
            jax.ShapeDtypeStruct((own_rows, head_width), BF16),
            jax.ShapeDtypeStruct((own_rows, head_width + STATS), F32),
            jax.ShapeDtypeStruct(group.shape[1:], BF16),
        ],
        in_specs=[VMEM] * 5,
        out_specs=[VMEM] * 4,
        compiler_params=pltpu.CompilerParams(vmem_limit_bytes=LIMIT * MIB),
        name="own",
    )(normed, queries, wk, wv, group)


def merge_kernel(places, n_landed, *refs):
    landed, (self_ref, wo_ref, part_ref, sent_ref) = refs[:n_landed], refs[n_landed:]
    head_width = wo_ref.shape[0]
    heads = head_width // HEAD_DIM
    self_scores = self_ref[:, head_width:]

    def left(x, n):
        return pltpu.roll(x, STATS - n, 1)

    stats = []
    for a, k in places:
        pieces = landed[a][k, :, head_width:].astype(F32)
        stats.append(pieces + left(pieces, 2 * heads) + left(pieces, 4 * heads))
    top = functools.reduce(jnp.maximum, stats, self_scores)
    self_weight = jnp.exp(self_scores - top)
    scales = [jnp.exp(stat - top) for stat in stats]
    total = self_weight
    for stat, scale in zip(stats, scales):
        total = total + scale * left(stat, heads)
    attended = []
    for h in range(heads):
        cols = slice(h * HEAD_DIM, (h + 1) * HEAD_DIM)
        summed = self_weight[:, h : h + 1] * self_ref[:, cols]
        for (a, k), scale in zip(places, scales):
            summed = summed + scale[:, h : h + 1] * landed[a][k, :, cols].astype(F32)
        attended.append((summed / total[:, h : h + 1]).astype(BF16))
    part = dot(jnp.concatenate(attended, axis=1), wo_ref[...])
    part_ref[...] = part
    sent_ref[...] = part.astype(BF16)


def merge(landed, self_part, wo):
    shape = (self_part.shape[0], wo.shape[1])
    return pl.pallas_call(
        functools.partial(merge_kernel, landed_blocks(lax.axis_size("req")), len(landed)),
        out_shape=(jax.ShapeDtypeStruct(shape, F32), jax.ShapeDtypeStruct(shape, BF16)),
        in_specs=[VMEM] * (len(landed) + 2),
        out_specs=(VMEM,) * 2,
        compiler_params=pltpu.CompilerParams(vmem_limit_bytes=16 * MIB),
        name="merge",
    )(*landed, self_part, wo)


def middle_kernel(*refs):
    part_ref, *others, tokens_ref, gain_ref, normed_ref, columns_ref, mid = refs
    column_width = columns_ref.shape[1]
    total = part_ref[...]
    for other in others:
        total = total + other[...].astype(F32)
    middle = tokens_ref[...].astype(F32) + total
    mid[...] = middle
    normed_ref[...] = layer_norm(middle, gain_ref[...]).astype(BF16)
    offset = pl.multiple_of(lax.axis_index("tp") * column_width, column_width)
    columns_ref[...] = mid[:, pl.ds(offset, column_width)]


def middle(part, others, tokens, gain):
    own_rows, width = tokens.shape
    return pl.pallas_call(
        middle_kernel,
        out_shape=(
            jax.ShapeDtypeStruct((own_rows, width), BF16),
            jax.ShapeDtypeStruct((own_rows, width // (1 + len(others))), F32),
        ),
        in_specs=[VMEM] * (3 + len(others)),
        out_specs=(VMEM,) * 2,
        scratch_shapes=[pltpu.VMEM((own_rows, width), F32)],
        compiler_params=pltpu.CompilerParams(vmem_limit_bytes=16 * MIB),
        name="middle",
    )(part, *others, tokens, gain)


def mlp_kernel(req_count, tp_count, n_normed, *refs):
    normed_refs, (up_ref, down_ref, up_peer_ref, down_peer_ref, out_ref) = refs[:n_normed], refs[n_normed:]
    own_rows, column_width = out_ref.shape[1:]
    me = lax.axis_index("req")
    normed = stacked(normed_refs).astype(BF16)
    order = term_order(req_count, tp_count)
    activations = []
    for ref in (up_ref, up_peer_ref):
        up = dot(normed, ref[...])
        activations.append((0.5 * up * (1.0 + lax.erf(up * 0.5**0.5))).astype(BF16))
    for t in range(tp_count):
        cols = slice(t * column_width, (t + 1) * column_width)
        term = dot(activations[0], down_ref[:, cols]) + dot(activations[1], down_peer_ref[:, cols])
        for c, offset in enumerate([0] + far_offsets(req_count)):
            chip, place = (me ^ offset) // 2, 0
            for other in range(req_count // 2):
                place = jnp.where(chip == other, order.index(other * tp_count + t), place)
            out_ref[place] = term[c * own_rows : (c + 1) * own_rows].astype(BF16)


def mlp(normed, *weights):
    req_count, tp_count = lax.axis_size("req"), lax.axis_size("tp")
    own_rows, width = normed[0].shape[1:]
    return pl.pallas_call(
        functools.partial(mlp_kernel, req_count, tp_count, len(normed)),
        out_shape=jax.ShapeDtypeStruct(
            (req_count * tp_count // 2, own_rows, width // tp_count), BF16
        ),
        in_specs=[VMEM] * (len(normed) + len(weights)),
        out_specs=VMEM,
        compiler_params=pltpu.CompilerParams(vmem_limit_bytes=16 * MIB),
        name="mlp",
    )(*normed, *weights)


def finish_kernel(recv_ref, columns_ref, out_ref):
    total = recv_ref[0].astype(F32)
    for k in range(1, recv_ref.shape[0]):
        total = total + recv_ref[k].astype(F32)
    out_ref[...] = (columns_ref[...] + total).astype(BF16)


def finish(recv, columns):
    return pl.pallas_call(
        finish_kernel,
        out_shape=jax.ShapeDtypeStruct(columns.shape, BF16),
        in_specs=[VMEM] * 2,
        out_specs=VMEM,
        compiler_params=pltpu.CompilerParams(vmem_limit_bytes=16 * MIB),
        name="finish",
    )(recv, columns)


def body(
    tokens,
    first_gain,
    query_weight,
    key_weight,
    value_weight,
    out_weight,
    second_gain,
    up_weight,
    down_weight,
    cache_keys,
    cache_values,
    lengths,
    stream_order,
):
    req_count = lax.axis_size("req")
    tp_count = lax.axis_size("tp")
    up_peer, down_peer = swap(up_weight, "req", 1), swap(down_weight, "req", 1)
    far = gather_far(tokens)
    tokens, gain, wq, first_keys, bounds = load(
        lengths[None],
        stream_order[None],
        tokens,
        first_gain[None],
        query_weight,
        cache_keys,
        last_rows=cache_keys.shape[0] * 3 // 4,
    )
    sends, own_normed, own_queries = attend(
        gather_near(tokens, far), gain, bounds, wq, first_keys, cache_keys, cache_values
    )
    new_keys, new_values, self_part, near = own_part(
        own_normed, own_queries, key_weight, value_weight, sends[0]
    )
    landed = scatter_far(sends)
    landed.append(scatter_near(near, landed[1:]))
    part, sent = merge(landed, self_part, out_weight)
    others = [swap(sent, "tp", m) for m in [tp_count - 1] + list(range(1, tp_count - 1))]
    normed, columns = middle(part, others, tokens, second_gain[None])
    all_normed = [part[None] for part in [normed] + gather_far(normed)]
    term = mlp(all_normed, up_weight, down_weight, up_peer, down_peer)
    order = term_order(req_count, tp_count)
    same_core = [
        [(2 * (k // tp_count) + core) * tp_count + k % tp_count for k in order]
        for core in range(2)
    ]
    terms = lax.all_to_all(
        term,
        ("req", "tp"),
        split_axis=0,
        concat_axis=0,
        tiled=True,
        axis_index_groups=same_core,
    )
    hidden = finish(terms, columns)
    return (hidden, new_keys, new_values)


def solution(mesh):
    return jax.shard_map(
        body,
        mesh=mesh,
        in_specs=(
            P("req", None),
            P(),
            P(None, "tp"),
            P(None, "tp"),
            P(None, "tp"),
            P("tp", None),
            P(),
            P(None, ("req", "tp")),
            P(("req", "tp"), None),
            P("req", "tp"),
            P("req", "tp"),
            P(),
            P(),
        ),
        out_specs=(P("req", "tp"), P("req", "tp"), P("req", "tp")),
        check_vma=False,
    )
```

```python
import functools

import jax
import jax.numpy as jnp
from jax import lax
from jax.experimental import pallas as pl
from jax.experimental.pallas import tpu as pltpu
from jax.sharding import PartitionSpec as P

HEAD_DIM = 128
STATS = 128
NONE = -1e30
CHUNK = 1024
MIB = 1 << 20
LIMIT = 8
VMEM = pl.BlockSpec(memory_space=pltpu.VMEM)
ANY = pl.BlockSpec(memory_space=pl.ANY)
F32 = jnp.float32
BF16 = jnp.bfloat16


def layer_norm(values, gain_vector):
    center = jnp.mean(values, axis=-1, keepdims=True)
    shifted = values - center
    spread = jnp.mean(shifted * shifted, axis=-1, keepdims=True)
    return shifted * lax.rsqrt(spread + 1e-05) * gain_vector


def dot(a, b):
    return jnp.dot(a, b, preferred_element_type=F32)


def stream_ranges(lens_row, order_row):
    n = lens_row.shape[1]
    down = lax.broadcasted_iota(jnp.int32, (n, n), 0)
    across = lax.broadcasted_iota(jnp.int32, (n, n), 1)
    lens = lens_row.astype(F32)
    eye = down == across
    lens_col = jnp.sum(jnp.where(eye, lens, 0.0), axis=1, keepdims=True)
    holds = order_row == down
    slot_len = jnp.sum(jnp.where(holds, lens_col, 0.0), axis=0, keepdims=True)
    slot_len_col = jnp.sum(jnp.where(eye, slot_len, 0.0), axis=1, keepdims=True)
    before = jnp.sum(jnp.where(down < across, slot_len_col, 0.0), axis=0, keepdims=True)
    first = jnp.sum(jnp.where(holds, before, 0.0), axis=1, keepdims=True)
    return first.astype(jnp.int32), (first + lens_col).astype(jnp.int32)


TERM_ORDER = (10, 11, 0, 2, 9, 14, 7, 4, 5, 6, 3, 13, 15, 8, 12, 1)


def term_order(req_count, tp_count):
    n = req_count * tp_count // 2
    return TERM_ORDER if n == len(TERM_ORDER) else tuple(range(n))


def swap(x, axis, offset):
    n = lax.axis_size(axis)
    return lax.ppermute(x, axis, [(i, i ^ offset) for i in range(n)])


def far_offsets(n):
    return list(range(n - 2, 0, -2))


def exchange_order(n):
    same = [0] + far_offsets(n)
    return same + [offset + 1 for offset in same]


def gather_far(x):
    return [swap(x, "req", m) for m in far_offsets(lax.axis_size("req"))]


def gather_near(x, far):
    return [x[None]] + [part[None] for part in far] + [swap(jnp.stack([x] + far), "req", 1)]


def scatter_far(groups):
    offsets = far_offsets(lax.axis_size("req"))
    return groups[:1] + [swap(group, "req", m) for group, m in zip(groups[1:], offsets)]


def scatter_near(near, far):
    return swap(jnp.stack([near] + [part[1] for part in far]), "req", 1)


def landed_blocks(n):
    return [(c, 0) for c in range(n // 2)] + [(n // 2, c) for c in range(n // 2)]


def split_three(x):
    parts = []
    for _ in range(3):
        parts.append(x.astype(BF16).astype(F32))
        x = x - parts[-1]
    return parts


def stacked(refs):
    blocks = [ref[k].astype(F32) for ref in refs for k in range(ref.shape[0])]
    return jnp.concatenate(blocks, axis=0)


def load_kernel(n, *refs):
    sources, targets = refs[:n], refs[n : 2 * n - 2]
    bounds_ref, lens, order, sems = refs[2 * n - 2 :]
    targets = (lens, order) + targets
    copies = [
        pltpu.make_async_copy(source.at[pl.ds(0, target.shape[0])], target, sems.at[k])
        for k, (source, target) in enumerate(zip(sources, targets))
    ]
    for copy in copies:
        copy.start()
    copies[0].wait()
    copies[1].wait()
    first, last = stream_ranges(lens[...], order[...])
    bounds_ref[0] = jnp.broadcast_to(first, bounds_ref.shape[1:])
    bounds_ref[1] = jnp.broadcast_to(last, bounds_ref.shape[1:])
    for copy in copies[2:]:
        copy.wait()


def load(lens, order, *arrays, last_rows):
    sources = [pltpu.with_memory_space_constraint(x, pltpu.HBM) for x in (lens, order) + arrays]
    last = arrays[-1]
    return pl.pallas_call(
        functools.partial(load_kernel, len(sources)),
        out_shape=[pltpu.VMEM(x.shape, x.dtype) for x in arrays[:-1]]
        + [pltpu.VMEM((last_rows, last.shape[1]), last.dtype)]
        + [pltpu.VMEM((2, lens.shape[1], 128), jnp.int32)],
        in_specs=[ANY] * len(sources),
        out_specs=[VMEM] * (len(arrays) + 1),
        scratch_shapes=[
            pltpu.VMEM(lens.shape, jnp.int32),
            pltpu.VMEM(order.shape, jnp.int32),
            pltpu.SemaphoreType.DMA((len(sources),)),
        ],
        compiler_params=pltpu.CompilerParams(vmem_limit_bytes=LIMIT * MIB),
        cost_estimate=pl.CostEstimate(
            flops=0, bytes_accessed=2 * sum(x.size for x in arrays), transcendentals=0
        ),
        name="load",
    )(*sources)


def attention_kernel(req_count, n_tokens, *refs):
    token_refs, refs = refs[:n_tokens], refs[n_tokens:]
    gain_ref, bounds, wq, first_keys, keys_hbm, values_hbm = refs[:6]
    groups = req_count // 2
    send_refs, refs = refs[6 : 6 + groups], refs[6 + groups :]
    own_normed_ref, own_queries_ref, last_keys, values, scores, sems = refs
    rows, head_width = values.shape
    held = first_keys.shape[0]
    heads = head_width // HEAD_DIM
    chunks = rows // CHUNK
    own_rows = own_normed_ref.shape[0] // 2
    requests = own_rows * req_count
    me = lax.axis_index("req")

    copies = []
    for c in range(held // CHUNK, chunks):
        there, here = pl.ds(c * CHUNK, CHUNK), pl.ds(c * CHUNK - held, CHUNK)
        copies.append(
            pltpu.make_async_copy(keys_hbm.at[there], last_keys.at[here], sems.at[len(copies)])
        )
    late = len(copies)
    for c in range(chunks):
        part = pl.ds(c * CHUNK, CHUNK)
        copies.append(
            pltpu.make_async_copy(values_hbm.at[part], values.at[part], sems.at[len(copies)])
        )
    for copy in copies:
        copy.start()
    normed = layer_norm(stacked(token_refs), gain_ref[...]).astype(BF16)
    owners = [
        pl.ds(pl.multiple_of((me ^ offset) * own_rows, own_rows), own_rows)
        for offset in exchange_order(req_count)
    ]
    first = jnp.concatenate([bounds[0, owner][:, :1] for owner in owners], axis=0) - me * rows
    last = jnp.concatenate([bounds[1, owner][:, :1] for owner in owners], axis=0) - me * rows
    queries = (dot(normed, wq[...]) * HEAD_DIM ** (-0.5)).astype(BF16)

    pairs = heads // 2
    two = 2 * requests
    wide = 2 * HEAD_DIM
    zero = jnp.zeros((requests, HEAD_DIM), BF16)
    paired = []
    for p in range(pairs):
        left = queries[:, p * wide : p * wide + HEAD_DIM]
        right = queries[:, p * wide + HEAD_DIM : (p + 1) * wide]
        upper = jnp.concatenate([left, zero], axis=1)
        lower = jnp.concatenate([zero, right], axis=1)
        paired.append(jnp.concatenate([upper, lower], axis=0))
    lane_max = [jnp.full((two, 128), NONE, F32)] * pairs
    for c in range(chunks):
        keys, at = first_keys, c * CHUNK
        if at >= held:
            copies[(at - held) // CHUNK].wait()
            keys, at = last_keys, at - held
        place = c * CHUNK + lax.broadcasted_iota(jnp.int32, (requests, CHUNK), 1)
        member = (place >= first) & (place < last)
        for p in range(pairs):
            score = lax.dot_general(
                paired[p],
                keys[at : at + CHUNK, p * wide : (p + 1) * wide],
                (((1,), (1,)), ((), ())),
                preferred_element_type=F32,
            )
            score = jnp.concatenate(
                [
                    jnp.where(member, score[:requests], NONE),
                    jnp.where(member, score[requests:], NONE),
                ],
                axis=0,
            )
            scores[p, :, c * CHUNK : (c + 1) * CHUNK] = score
            for t in range(CHUNK // 128):
                lane_max[p] = jnp.maximum(lane_max[p], score[:, t * 128 : (t + 1) * 128])

    tops = [jnp.max(lane_max[p], axis=1, keepdims=True) for p in range(pairs)]
    sums = [jnp.zeros((two, 128), F32)] * pairs
    outs = [jnp.zeros((two, wide), F32)] * pairs
    for c in range(chunks):
        copies[late + c].wait()
        for p in range(pairs):
            expo = jnp.exp(scores[p, :, c * CHUNK : (c + 1) * CHUNK] - tops[p])
            for t in range(CHUNK // 128):
                sums[p] = sums[p] + expo[:, t * 128 : (t + 1) * 128]
            outs[p] = outs[p] + dot(
                expo.astype(BF16),
                values[c * CHUNK : (c + 1) * CHUNK, p * wide : (p + 1) * wide],
            )
    peak, mass, partial = [], [], []
    for h in range(heads):
        p, r = h // 2, slice(h % 2 * requests, (h % 2 + 1) * requests)
        peak.append(tops[p][r])
        mass.append(sums[p][r])
        partial.append(outs[p][r, h % 2 * HEAD_DIM : (h % 2 + 1) * HEAD_DIM])
    lane = lax.broadcasted_iota(jnp.int32, (requests, STATS), 1)
    stats = jnp.zeros((requests, STATS), F32)
    for h in range(heads):
        both = (peak[h], jnp.sum(mass[h], axis=1, keepdims=True))
        for kind, number in enumerate(both):
            for k, piece in enumerate(split_three(number)):
                stats = jnp.where(lane == (k * 2 + kind) * heads + h, piece, stats)
    for c, ref in enumerate(send_refs):
        for k, block in enumerate((c, groups + c)):
            r = slice(block * own_rows, (block + 1) * own_rows)
            for h in range(heads):
                ref[k, :, h * HEAD_DIM : (h + 1) * HEAD_DIM] = partial[h][r].astype(BF16)
            ref[k, :, head_width : head_width + STATS] = stats[r].astype(BF16)
    own_normed_ref[...] = normed[: 2 * own_rows]
    own_queries_ref[...] = queries[: 2 * own_rows].astype(F32)


def attend(tokens, gain, bounds, wq, first_keys, keys, values):
    req_count = lax.axis_size("req")
    own_rows, width = tokens[0].shape[1:]
    requests = own_rows * req_count
    rows, head_width = keys.shape
    heads = head_width // HEAD_DIM
    groups = req_count // 2
    scratch = heads * requests * rows * 4 + 4 * rows * head_width
    *sends, own_normed, own_queries = pl.pallas_call(
        functools.partial(attention_kernel, req_count, len(tokens)),
        out_shape=[jax.ShapeDtypeStruct((2, own_rows, head_width + STATS), BF16)] * groups
        + [
            jax.ShapeDtypeStruct((2 * own_rows, width), BF16),
            jax.ShapeDtypeStruct((2 * own_rows, head_width), F32),
        ],
        in_specs=[VMEM] * (len(tokens) + 4) + [ANY] * 2,
        out_specs=[VMEM] * (groups + 2),
        scratch_shapes=[
            pltpu.VMEM((rows - first_keys.shape[0], head_width), BF16),
            pltpu.VMEM((rows, head_width), BF16),
            pltpu.VMEM((heads // 2, 2 * requests, rows), F32),
            pltpu.SemaphoreType.DMA((2 * rows // CHUNK,)),
        ],
        compiler_params=pltpu.CompilerParams(vmem_limit_bytes=scratch + LIMIT * MIB),
        name="attention",
    )(
        *tokens,
        gain,
        bounds,
        wq,
        first_keys,
        pltpu.with_memory_space_constraint(keys, pltpu.HBM),
        pltpu.with_memory_space_constraint(values, pltpu.HBM),
    )
    return sends, own_normed, own_queries


def own_kernel(normed_ref, queries_ref, wk, wv, group_ref, new_keys_ref, new_values_ref, self_ref, near_ref):
    own_rows, head_width = new_keys_ref.shape
    new_keys = dot(normed_ref[...], wk[...])[:own_rows].astype(BF16)
    new_values = dot(normed_ref[...], wv[...])[:own_rows].astype(BF16)
    new_keys_ref[...] = new_keys
    new_values_ref[...] = new_values
    product = queries_ref[:own_rows] * new_keys.astype(F32)
    lane = lax.broadcasted_iota(jnp.int32, (own_rows, STATS), 1)
    self_score = jnp.zeros((own_rows, STATS), F32)
    for h in range(head_width // HEAD_DIM):
        one = jnp.sum(product[:, h * HEAD_DIM : (h + 1) * HEAD_DIM], axis=1, keepdims=True)
        self_score = jnp.where(lane == h, one, self_score)
    self_ref[:, :head_width] = new_values.astype(F32)
    self_ref[:, head_width:] = self_score
    near_ref[...] = group_ref[1]


def own_part(normed, queries, wk, wv, group):
    own_rows, head_width = normed.shape[0] // 2, wk.shape[1]
    return pl.pallas_call(
        own_kernel,
        out_shape=[
            jax.ShapeDtypeStruct((own_rows, head_width), BF16),
            jax.ShapeDtypeStruct((own_rows, head_width), BF16),
            jax.ShapeDtypeStruct((own_rows, head_width + STATS), F32),
            jax.ShapeDtypeStruct(group.shape[1:], BF16),
        ],
        in_specs=[VMEM] * 5,
        out_specs=[VMEM] * 4,
        compiler_params=pltpu.CompilerParams(vmem_limit_bytes=LIMIT * MIB),
        name="own",
    )(normed, queries, wk, wv, group)


def merge_kernel(places, n_landed, *refs):
    landed, (self_ref, wo_ref, part_ref, sent_ref) = refs[:n_landed], refs[n_landed:]
    head_width = wo_ref.shape[0]
    heads = head_width // HEAD_DIM
    self_scores = self_ref[:, head_width:]

    def left(x, n):
        return pltpu.roll(x, STATS - n, 1)

    stats = []
    for a, k in places:
        pieces = landed[a][k, :, head_width:].astype(F32)
        stats.append(pieces + left(pieces, 2 * heads) + left(pieces, 4 * heads))
    top = functools.reduce(jnp.maximum, stats, self_scores)
    self_weight = jnp.exp(self_scores - top)
    scales = [jnp.exp(stat - top) for stat in stats]
    total = self_weight
    for stat, scale in zip(stats, scales):
        total = total + scale * left(stat, heads)
    attended = []
    for h in range(heads):
        cols = slice(h * HEAD_DIM, (h + 1) * HEAD_DIM)
        summed = self_weight[:, h : h + 1] * self_ref[:, cols]
        for (a, k), scale in zip(places, scales):
            summed = summed + scale[:, h : h + 1] * landed[a][k, :, cols].astype(F32)
        attended.append((summed / total[:, h : h + 1]).astype(BF16))
    part = dot(jnp.concatenate(attended, axis=1), wo_ref[...])
    part_ref[...] = part
    sent_ref[...] = part.astype(BF16)


def merge(landed, self_part, wo):
    shape = (self_part.shape[0], wo.shape[1])
    return pl.pallas_call(
        functools.partial(merge_kernel, landed_blocks(lax.axis_size("req")), len(landed)),
        out_shape=(jax.ShapeDtypeStruct(shape, F32), jax.ShapeDtypeStruct(shape, BF16)),
        in_specs=[VMEM] * (len(landed) + 2),
        out_specs=(VMEM,) * 2,
        compiler_params=pltpu.CompilerParams(vmem_limit_bytes=16 * MIB),
        name="merge",
    )(*landed, self_part, wo)


def middle_kernel(*refs):
    part_ref, *others, tokens_ref, gain_ref, normed_ref, columns_ref, mid = refs
    column_width = columns_ref.shape[1]
    total = part_ref[...]
    for other in others:
        total = total + other[...].astype(F32)
    middle = tokens_ref[...].astype(F32) + total
    mid[...] = middle
    normed_ref[...] = layer_norm(middle, gain_ref[...]).astype(BF16)
    offset = pl.multiple_of(lax.axis_index("tp") * column_width, column_width)
    columns_ref[...] = mid[:, pl.ds(offset, column_width)]


def middle(part, others, tokens, gain):
    own_rows, width = tokens.shape
    return pl.pallas_call(
        middle_kernel,
        out_shape=(
            jax.ShapeDtypeStruct((own_rows, width), BF16),
            jax.ShapeDtypeStruct((own_rows, width // (1 + len(others))), F32),
        ),
        in_specs=[VMEM] * (3 + len(others)),
        out_specs=(VMEM,) * 2,
        scratch_shapes=[pltpu.VMEM((own_rows, width), F32)],
        compiler_params=pltpu.CompilerParams(vmem_limit_bytes=16 * MIB),
        name="middle",
    )(part, *others, tokens, gain)


def mlp_kernel(req_count, tp_count, n_normed, *refs):
    normed_refs, (up_ref, down_ref, up_peer_ref, down_peer_ref, out_ref) = refs[:n_normed], refs[n_normed:]
    own_rows, column_width = out_ref.shape[1:]
    me = lax.axis_index("req")
    normed = stacked(normed_refs).astype(BF16)
    order = term_order(req_count, tp_count)
    activations = []
    for ref in (up_ref, up_peer_ref):
        up = dot(normed, ref[...])
        activations.append((0.5 * up * (1.0 + lax.erf(up * 0.5**0.5))).astype(BF16))
    for t in range(tp_count):
        cols = slice(t * column_width, (t + 1) * column_width)
        term = dot(activations[0], down_ref[:, cols]) + dot(activations[1], down_peer_ref[:, cols])
        for c, offset in enumerate([0] + far_offsets(req_count)):
            chip, place = (me ^ offset) // 2, 0
            for other in range(req_count // 2):
                place = jnp.where(chip == other, order.index(other * tp_count + t), place)
            out_ref[place] = term[c * own_rows : (c + 1) * own_rows].astype(BF16)


def mlp(normed, *weights):
    req_count, tp_count = lax.axis_size("req"), lax.axis_size("tp")
    own_rows, width = normed[0].shape[1:]
    return pl.pallas_call(
        functools.partial(mlp_kernel, req_count, tp_count, len(normed)),
        out_shape=jax.ShapeDtypeStruct(
            (req_count * tp_count // 2, own_rows, width // tp_count), BF16
        ),
        in_specs=[VMEM] * (len(normed) + len(weights)),
        out_specs=VMEM,
        compiler_params=pltpu.CompilerParams(vmem_limit_bytes=16 * MIB),
        name="mlp",
    )(*normed, *weights)


def finish_kernel(recv_ref, columns_ref, out_ref):
    total = recv_ref[0].astype(F32)
    for k in range(1, recv_ref.shape[0]):
        total = total + recv_ref[k].astype(F32)
    out_ref[...] = (columns_ref[...] + total).astype(BF16)


def finish(recv, columns):
    return pl.pallas_call(
        finish_kernel,
        out_shape=jax.ShapeDtypeStruct(columns.shape, BF16),
        in_specs=[VMEM] * 2,
        out_specs=VMEM,
        compiler_params=pltpu.CompilerParams(vmem_limit_bytes=16 * MIB),
        name="finish",
    )(recv, columns)


def body(
    tokens,
    first_gain,
    query_weight,
    key_weight,
    value_weight,
    out_weight,
    second_gain,
    up_weight,
    down_weight,
    cache_keys,
    cache_values,
    lengths,
    stream_order,
):
    req_count = lax.axis_size("req")
    tp_count = lax.axis_size("tp")
    up_peer, down_peer = swap(up_weight, "req", 1), swap(down_weight, "req", 1)
    far = gather_far(tokens)
    tokens, gain, wq, first_keys, bounds = load(
        lengths[None],
        stream_order[None],
        tokens,
        first_gain[None],
        query_weight,
        cache_keys,
        last_rows=cache_keys.shape[0] * 3 // 4,
    )
    sends, own_normed, own_queries = attend(
        gather_near(tokens, far), gain, bounds, wq, first_keys, cache_keys, cache_values
    )
    new_keys, new_values, self_part, near = own_part(
        own_normed, own_queries, key_weight, value_weight, sends[0]
    )
    landed = scatter_far(sends)
    landed.append(scatter_near(near, landed[1:]))
    part, sent = merge(landed, self_part, out_weight)
    others = [swap(sent, "tp", m) for m in [tp_count - 1] + list(range(1, tp_count - 1))]
    normed, columns = middle(part, others, tokens, second_gain[None])
    all_normed = [part[None] for part in [normed] + gather_far(normed)]
    term = mlp(all_normed, up_weight, down_weight, up_peer, down_peer)
    order = term_order(req_count, tp_count)
    same_core = [
        [(2 * (k // tp_count) + core) * tp_count + k % tp_count for k in order]
        for core in range(2)
    ]
    terms = lax.all_to_all(
        term,
        ("req", "tp"),
        split_axis=0,
        concat_axis=0,
        tiled=True,
        axis_index_groups=same_core,
    )
    hidden = finish(terms, columns)
    return (hidden, new_keys, new_values)


def solution(mesh):
    return jax.shard_map(
        body,
        mesh=mesh,
        in_specs=(
            P("req", None),
            P(),
            P(None, "tp"),
            P(None, "tp"),
            P(None, "tp"),
            P("tp", None),
            P(),
            P(None, ("req", "tp")),
            P(("req", "tp"), None),
            P("req", "tp"),
            P("req", "tp"),
            P(),
            P(),
        ),
        out_specs=(P("req", "tp"), P("req", "tp"), P("req", "tp")),
        check_vma=False,
    )
```

```python
import functools

import jax
import jax.numpy as jnp
from jax import lax
from jax.experimental import pallas as pl
from jax.experimental.pallas import tpu as pltpu
from jax.sharding import PartitionSpec as P

HEAD_DIM = 128
STATS = 128
NONE = -1e30
CHUNK = 1024
MIB = 1 << 20
LIMIT = 8
VMEM = pl.BlockSpec(memory_space=pltpu.VMEM)
ANY = pl.BlockSpec(memory_space=pl.ANY)
F32 = jnp.float32
BF16 = jnp.bfloat16


def layer_norm(values, gain_vector):
    center = jnp.mean(values, axis=-1, keepdims=True)
    shifted = values - center
    spread = jnp.mean(shifted * shifted, axis=-1, keepdims=True)
    return shifted * lax.rsqrt(spread + 1e-05) * gain_vector


def dot(a, b):
    return jnp.dot(a, b, preferred_element_type=F32)


def stream_ranges(lens_row, order_row):
    n = lens_row.shape[1]
    down = lax.broadcasted_iota(jnp.int32, (n, n), 0)
    across = lax.broadcasted_iota(jnp.int32, (n, n), 1)
    lens = lens_row.astype(F32)
    eye = down == across
    lens_col = jnp.sum(jnp.where(eye, lens, 0.0), axis=1, keepdims=True)
    holds = order_row == down
    slot_len = jnp.sum(jnp.where(holds, lens_col, 0.0), axis=0, keepdims=True)
    slot_len_col = jnp.sum(jnp.where(eye, slot_len, 0.0), axis=1, keepdims=True)
    before = jnp.sum(jnp.where(down < across, slot_len_col, 0.0), axis=0, keepdims=True)
    first = jnp.sum(jnp.where(holds, before, 0.0), axis=1, keepdims=True)
    return first.astype(jnp.int32), (first + lens_col).astype(jnp.int32)


TERM_ORDER = (10, 11, 0, 2, 9, 14, 7, 4, 5, 6, 3, 13, 15, 8, 12, 1)


def term_order(req_count, tp_count):
    n = req_count * tp_count // 2
    return TERM_ORDER if n == len(TERM_ORDER) else tuple(range(n))


def swap(x, axis, offset):
    n = lax.axis_size(axis)
    return lax.ppermute(x, axis, [(i, i ^ offset) for i in range(n)])


def far_offsets(n):
    return list(range(n - 2, 0, -2))


def exchange_order(n):
    same = [0] + far_offsets(n)
    return same + [offset + 1 for offset in same]


def gather_far(x):
    return [swap(x, "req", m) for m in far_offsets(lax.axis_size("req"))]


def gather_near(x, far):
    return [x[None]] + [part[None] for part in far] + [swap(jnp.stack([x] + far), "req", 1)]


def scatter_far(groups):
    offsets = far_offsets(lax.axis_size("req"))
    return groups[:1] + [swap(group, "req", m) for group, m in zip(groups[1:], offsets)]


def scatter_near(near, far):
    return swap(jnp.stack([near] + [part[1] for part in far]), "req", 1)


def landed_blocks(n):
    return [(c, 0) for c in range(n // 2)] + [(n // 2, c) for c in range(n // 2)]


def split_three(x):
    parts = []
    for _ in range(3):
        parts.append(x.astype(BF16).astype(F32))
        x = x - parts[-1]
    return parts


def stacked(refs):
    blocks = [ref[k].astype(F32) for ref in refs for k in range(ref.shape[0])]
    return jnp.concatenate(blocks, axis=0)


def load_kernel(n, *refs):
    sources, targets = refs[:n], refs[n : 2 * n - 2]
    bounds_ref, lens, order, sems = refs[2 * n - 2 :]
    targets = (lens, order) + targets
    copies = [
        pltpu.make_async_copy(
            source if source.shape == target.shape else source.at[pl.ds(0, target.shape[0])],
            target,
            sems.at[k],
        )
        for k, (source, target) in enumerate(zip(sources, targets))
    ]
    for copy in copies:
        copy.start()
    copies[0].wait()
    copies[1].wait()
    first, last = stream_ranges(lens[...], order[...])
    bounds_ref[0] = jnp.broadcast_to(first, bounds_ref.shape[1:])
    bounds_ref[1] = jnp.broadcast_to(last, bounds_ref.shape[1:])
    for copy in copies[2:]:
        copy.wait()


def load(lens, order, *arrays, last_rows):
    sources = [pltpu.with_memory_space_constraint(x, pltpu.HBM) for x in (lens, order) + arrays]
    last = arrays[-1]
    return pl.pallas_call(
        functools.partial(load_kernel, len(sources)),
        out_shape=[pltpu.VMEM(x.shape, x.dtype) for x in arrays[:-1]]
        + [pltpu.VMEM((last_rows, last.shape[1]), last.dtype)]
        + [pltpu.VMEM((2, lens.shape[1], 128), jnp.int32)],
        in_specs=[ANY] * len(sources),
        out_specs=[VMEM] * (len(arrays) + 1),
        scratch_shapes=[
            pltpu.VMEM(lens.shape, jnp.int32),
            pltpu.VMEM(order.shape, jnp.int32),
            pltpu.SemaphoreType.DMA((len(sources),)),
        ],
        compiler_params=pltpu.CompilerParams(vmem_limit_bytes=LIMIT * MIB),
        cost_estimate=pl.CostEstimate(
            flops=0, bytes_accessed=2 * sum(x.size for x in arrays), transcendentals=0
        ),
        name="load",
    )(*sources)


def attention_kernel(req_count, n_tokens, *refs):
    token_refs, refs = refs[:n_tokens], refs[n_tokens:]
    gain_ref, bounds, wq, first_keys, keys_hbm, values_hbm = refs[:6]
    groups = req_count // 2
    send_refs, refs = refs[6 : 6 + groups], refs[6 + groups :]
    own_normed_ref, own_queries_ref, last_keys, values, scores, sems = refs
    rows, head_width = values.shape
    held = first_keys.shape[0]
    heads = head_width // HEAD_DIM
    chunks = rows // CHUNK
    own_rows = own_normed_ref.shape[0] // 2
    requests = own_rows * req_count
    me = lax.axis_index("req")

    copies = []
    for c in range(held // CHUNK, chunks):
        there, here = pl.ds(c * CHUNK, CHUNK), pl.ds(c * CHUNK - held, CHUNK)
        copies.append(
            pltpu.make_async_copy(keys_hbm.at[there], last_keys.at[here], sems.at[len(copies)])
        )
    late = len(copies)
    for c in range(chunks):
        part = pl.ds(c * CHUNK, CHUNK)
        copies.append(
            pltpu.make_async_copy(values_hbm.at[part], values.at[part], sems.at[len(copies)])
        )
    for copy in copies:
        copy.start()
    normed = layer_norm(stacked(token_refs), gain_ref[...]).astype(BF16)
    owners = [
        pl.ds(pl.multiple_of((me ^ offset) * own_rows, own_rows), own_rows)
        for offset in exchange_order(req_count)
    ]
    first = jnp.concatenate([bounds[0, owner][:, :1] for owner in owners], axis=0) - me * rows
    last = jnp.concatenate([bounds[1, owner][:, :1] for owner in owners], axis=0) - me * rows
    queries = (dot(normed, wq[...]) * HEAD_DIM ** (-0.5)).astype(BF16)

    pairs = heads // 2
    two = 2 * requests
    wide = 2 * HEAD_DIM
    zero = jnp.zeros((requests, HEAD_DIM), BF16)
    paired = []
    for p in range(pairs):
        left = queries[:, p * wide : p * wide + HEAD_DIM]
        right = queries[:, p * wide + HEAD_DIM : (p + 1) * wide]
        upper = jnp.concatenate([left, zero], axis=1)
        lower = jnp.concatenate([zero, right], axis=1)
        paired.append(jnp.concatenate([upper, lower], axis=0))
    lane_max = [jnp.full((two, 128), NONE, F32)] * pairs
    for c in range(chunks):
        keys, at = first_keys, c * CHUNK
        if at >= held:
            copies[(at - held) // CHUNK].wait()
            keys, at = last_keys, at - held
        place = c * CHUNK + lax.broadcasted_iota(jnp.int32, (requests, CHUNK), 1)
        member = (place >= first) & (place < last)
        for p in range(pairs):
            score = lax.dot_general(
                paired[p],
                keys[at : at + CHUNK, p * wide : (p + 1) * wide],
                (((1,), (1,)), ((), ())),
                preferred_element_type=F32,
            )
            score = jnp.concatenate(
                [
                    jnp.where(member, score[:requests], NONE),
                    jnp.where(member, score[requests:], NONE),
                ],
                axis=0,
            )
            scores[p, :, c * CHUNK : (c + 1) * CHUNK] = score
            for t in range(CHUNK // 128):
                lane_max[p] = jnp.maximum(lane_max[p], score[:, t * 128 : (t + 1) * 128])

    tops = [jnp.max(lane_max[p], axis=1, keepdims=True) for p in range(pairs)]
    sums = [jnp.zeros((two, 128), F32)] * pairs
    outs = [jnp.zeros((two, wide), F32)] * pairs
    for c in range(chunks):
        copies[late + c].wait()
        for p in range(pairs):
            expo = jnp.exp(scores[p, :, c * CHUNK : (c + 1) * CHUNK] - tops[p])
            for t in range(CHUNK // 128):
                sums[p] = sums[p] + expo[:, t * 128 : (t + 1) * 128]
            outs[p] = outs[p] + dot(
                expo.astype(BF16),
                values[c * CHUNK : (c + 1) * CHUNK, p * wide : (p + 1) * wide],
            )
    peak, mass, partial = [], [], []
    for h in range(heads):
        p, r = h // 2, slice(h % 2 * requests, (h % 2 + 1) * requests)
        peak.append(tops[p][r])
        mass.append(sums[p][r])
        partial.append(outs[p][r, h % 2 * HEAD_DIM : (h % 2 + 1) * HEAD_DIM])
    lane = lax.broadcasted_iota(jnp.int32, (requests, STATS), 1)
    stats = jnp.zeros((requests, STATS), F32)
    for h in range(heads):
        both = (peak[h], jnp.sum(mass[h], axis=1, keepdims=True))
        for kind, number in enumerate(both):
            for k, piece in enumerate(split_three(number)):
                stats = jnp.where(lane == (k * 2 + kind) * heads + h, piece, stats)
    for c, ref in enumerate(send_refs):
        for k, block in enumerate((c, groups + c)):
            r = slice(block * own_rows, (block + 1) * own_rows)
            for h in range(heads):
                ref[k, :, h * HEAD_DIM : (h + 1) * HEAD_DIM] = partial[h][r].astype(BF16)
            ref[k, :, head_width : head_width + STATS] = stats[r].astype(BF16)
    own_normed_ref[...] = normed[: 2 * own_rows]
    own_queries_ref[...] = queries[: 2 * own_rows].astype(F32)


def attend(tokens, gain, bounds, wq, first_keys, keys, values):
    req_count = lax.axis_size("req")
    own_rows, width = tokens[0].shape[1:]
    requests = own_rows * req_count
    rows, head_width = keys.shape
    heads = head_width // HEAD_DIM
    groups = req_count // 2
    scratch = heads * requests * rows * 4 + 4 * rows * head_width
    *sends, own_normed, own_queries = pl.pallas_call(
        functools.partial(attention_kernel, req_count, len(tokens)),
        out_shape=[jax.ShapeDtypeStruct((2, own_rows, head_width + STATS), BF16)] * groups
        + [
            jax.ShapeDtypeStruct((2 * own_rows, width), BF16),
            jax.ShapeDtypeStruct((2 * own_rows, head_width), F32),
        ],
        in_specs=[VMEM] * (len(tokens) + 4) + [ANY] * 2,
        out_specs=[VMEM] * (groups + 2),
        scratch_shapes=[
            pltpu.VMEM((rows - first_keys.shape[0], head_width), BF16),
            pltpu.VMEM((rows, head_width), BF16),
            pltpu.VMEM((heads // 2, 2 * requests, rows), F32),
            pltpu.SemaphoreType.DMA((2 * rows // CHUNK,)),
        ],
        compiler_params=pltpu.CompilerParams(vmem_limit_bytes=scratch + LIMIT * MIB),
        name="attention",
    )(
        *tokens,
        gain,
        bounds,
        wq,
        first_keys,
        pltpu.with_memory_space_constraint(keys, pltpu.HBM),
        pltpu.with_memory_space_constraint(values, pltpu.HBM),
    )
    return sends, own_normed, own_queries


def own_kernel(normed_ref, queries_ref, wk, wv, group_ref, new_keys_ref, new_values_ref, self_ref, near_ref):
    own_rows, head_width = new_keys_ref.shape
    new_keys = dot(normed_ref[...], wk[...])[:own_rows].astype(BF16)
    new_values = dot(normed_ref[...], wv[...])[:own_rows].astype(BF16)
    new_keys_ref[...] = new_keys
    new_values_ref[...] = new_values
    product = queries_ref[:own_rows] * new_keys.astype(F32)
    lane = lax.broadcasted_iota(jnp.int32, (own_rows, STATS), 1)
    self_score = jnp.zeros((own_rows, STATS), F32)
    for h in range(head_width // HEAD_DIM):
        one = jnp.sum(product[:, h * HEAD_DIM : (h + 1) * HEAD_DIM], axis=1, keepdims=True)
        self_score = jnp.where(lane == h, one, self_score)
    self_ref[:, :head_width] = new_values.astype(F32)
    self_ref[:, head_width:] = self_score
    near_ref[...] = group_ref[1]


def own_part(normed, queries, wk, wv, group):
    own_rows, head_width = normed.shape[0] // 2, wk.shape[1]
    return pl.pallas_call(
        own_kernel,
        out_shape=[
            jax.ShapeDtypeStruct((own_rows, head_width), BF16),
            jax.ShapeDtypeStruct((own_rows, head_width), BF16),
            jax.ShapeDtypeStruct((own_rows, head_width + STATS), F32),
            jax.ShapeDtypeStruct(group.shape[1:], BF16),
        ],
        in_specs=[VMEM] * 5,
        out_specs=[VMEM] * 4,
        compiler_params=pltpu.CompilerParams(vmem_limit_bytes=LIMIT * MIB),
        name="own",
    )(normed, queries, wk, wv, group)


def merge_kernel(places, n_landed, *refs):
    landed, (self_ref, wo_ref, part_ref, sent_ref) = refs[:n_landed], refs[n_landed:]
    head_width = wo_ref.shape[0]
    heads = head_width // HEAD_DIM
    self_scores = self_ref[:, head_width:]

    def left(x, n):
        return pltpu.roll(x, STATS - n, 1)

    stats = []
    for a, k in places:
        pieces = landed[a][k, :, head_width:].astype(F32)
        stats.append(pieces + left(pieces, 2 * heads) + left(pieces, 4 * heads))
    top = functools.reduce(jnp.maximum, stats, self_scores)
    self_weight = jnp.exp(self_scores - top)
    scales = [jnp.exp(stat - top) for stat in stats]
    total = self_weight
    for stat, scale in zip(stats, scales):
        total = total + scale * left(stat, heads)
    attended = []
    for h in range(heads):
        cols = slice(h * HEAD_DIM, (h + 1) * HEAD_DIM)
        summed = self_weight[:, h : h + 1] * self_ref[:, cols]
        for (a, k), scale in zip(places, scales):
            summed = summed + scale[:, h : h + 1] * landed[a][k, :, cols].astype(F32)
        attended.append((summed / total[:, h : h + 1]).astype(BF16))
    part = dot(jnp.concatenate(attended, axis=1), wo_ref[...])
    part_ref[...] = part
    sent_ref[...] = part.astype(BF16)


def merge(landed, self_part, wo):
    shape = (self_part.shape[0], wo.shape[1])
    return pl.pallas_call(
        functools.partial(merge_kernel, landed_blocks(lax.axis_size("req")), len(landed)),
        out_shape=(jax.ShapeDtypeStruct(shape, F32), jax.ShapeDtypeStruct(shape, BF16)),
        in_specs=[VMEM] * (len(landed) + 2),
        out_specs=(VMEM,) * 2,
        compiler_params=pltpu.CompilerParams(vmem_limit_bytes=16 * MIB),
        name="merge",
    )(*landed, self_part, wo)


def middle_kernel(*refs):
    part_ref, *others, tokens_ref, gain_ref, normed_ref, columns_ref, mid = refs
    column_width = columns_ref.shape[1]
    total = part_ref[...]
    for other in others:
        total = total + other[...].astype(F32)
    middle = tokens_ref[...].astype(F32) + total
    mid[...] = middle
    normed_ref[...] = layer_norm(middle, gain_ref[...]).astype(BF16)
    offset = pl.multiple_of(lax.axis_index("tp") * column_width, column_width)
    columns_ref[...] = mid[:, pl.ds(offset, column_width)]


def middle(part, others, tokens, gain):
    own_rows, width = tokens.shape
    return pl.pallas_call(
        middle_kernel,
        out_shape=(
            jax.ShapeDtypeStruct((own_rows, width), BF16),
            jax.ShapeDtypeStruct((own_rows, width // (1 + len(others))), F32),
        ),
        in_specs=[VMEM] * (3 + len(others)),
        out_specs=(VMEM,) * 2,
        scratch_shapes=[pltpu.VMEM((own_rows, width), F32)],
        compiler_params=pltpu.CompilerParams(vmem_limit_bytes=16 * MIB),
        name="middle",
    )(part, *others, tokens, gain)


def mlp_kernel(req_count, tp_count, n_normed, *refs):
    normed_refs, (up_ref, down_ref, up_peer_ref, down_peer_ref, out_ref) = refs[:n_normed], refs[n_normed:]
    own_rows, column_width = out_ref.shape[1:]
    me = lax.axis_index("req")
    normed = stacked(normed_refs).astype(BF16)
    order = term_order(req_count, tp_count)
    activations = []
    for ref in (up_ref, up_peer_ref):
        up = dot(normed, ref[...])
        activations.append((0.5 * up * (1.0 + lax.erf(up * 0.5**0.5))).astype(BF16))
    for t in range(tp_count):
        cols = slice(t * column_width, (t + 1) * column_width)
        term = dot(activations[0], down_ref[:, cols]) + dot(activations[1], down_peer_ref[:, cols])
        for c, offset in enumerate([0] + far_offsets(req_count)):
            chip, place = (me ^ offset) // 2, 0
            for other in range(req_count // 2):
                place = jnp.where(chip == other, order.index(other * tp_count + t), place)
            out_ref[place] = term[c * own_rows : (c + 1) * own_rows].astype(BF16)


def mlp(normed, *weights):
    req_count, tp_count = lax.axis_size("req"), lax.axis_size("tp")
    own_rows, width = normed[0].shape[1:]
    return pl.pallas_call(
        functools.partial(mlp_kernel, req_count, tp_count, len(normed)),
        out_shape=jax.ShapeDtypeStruct(
            (req_count * tp_count // 2, own_rows, width // tp_count), BF16
        ),
        in_specs=[VMEM] * (len(normed) + len(weights)),
        out_specs=VMEM,
        compiler_params=pltpu.CompilerParams(vmem_limit_bytes=16 * MIB),
        name="mlp",
    )(*normed, *weights)


def finish_kernel(recv_ref, columns_ref, out_ref):
    total = recv_ref[0].astype(F32)
    for k in range(1, recv_ref.shape[0]):
        total = total + recv_ref[k].astype(F32)
    out_ref[...] = (columns_ref[...] + total).astype(BF16)


def finish(recv, columns):
    return pl.pallas_call(
        finish_kernel,
        out_shape=jax.ShapeDtypeStruct(columns.shape, BF16),
        in_specs=[VMEM] * 2,
        out_specs=VMEM,
        compiler_params=pltpu.CompilerParams(vmem_limit_bytes=16 * MIB),
        name="finish",
    )(recv, columns)


def body(
    tokens,
    first_gain,
    query_weight,
    key_weight,
    value_weight,
    out_weight,
    second_gain,
    up_weight,
    down_weight,
    cache_keys,
    cache_values,
    lengths,
    stream_order,
):
    req_count = lax.axis_size("req")
    tp_count = lax.axis_size("tp")
    up_peer, down_peer = swap(up_weight, "req", 1), swap(down_weight, "req", 1)
    far = gather_far(tokens)
    tokens, gain, wq, first_keys, bounds = load(
        lengths[None],
        stream_order[None],
        tokens,
        first_gain[None],
        query_weight,
        cache_keys,
        last_rows=cache_keys.shape[0] * 3 // 4,
    )
    sends, own_normed, own_queries = attend(
        gather_near(tokens, far), gain, bounds, wq, first_keys, cache_keys, cache_values
    )
    new_keys, new_values, self_part, near = own_part(
        own_normed, own_queries, key_weight, value_weight, sends[0]
    )
    landed = scatter_far(sends)
    landed.append(scatter_near(near, landed[1:]))
    part, sent = merge(landed, self_part, out_weight)
    others = [swap(sent, "tp", m) for m in [tp_count - 1] + list(range(1, tp_count - 1))]
    normed, columns = middle(part, others, tokens, second_gain[None])
    all_normed = [part[None] for part in [normed] + gather_far(normed)]
    term = mlp(all_normed, up_weight, down_weight, up_peer, down_peer)
    order = term_order(req_count, tp_count)
    same_core = [
        [(2 * (k // tp_count) + core) * tp_count + k % tp_count for k in order]
        for core in range(2)
    ]
    terms = lax.all_to_all(
        term,
        ("req", "tp"),
        split_axis=0,
        concat_axis=0,
        tiled=True,
        axis_index_groups=same_core,
    )
    hidden = finish(terms, columns)
    return (hidden, new_keys, new_values)


def solution(mesh):
    return jax.shard_map(
        body,
        mesh=mesh,
        in_specs=(
            P("req", None),
            P(),
            P(None, "tp"),
            P(None, "tp"),
            P(None, "tp"),
            P("tp", None),
            P(),
            P(None, ("req", "tp")),
            P(("req", "tp"), None),
            P("req", "tp"),
            P("req", "tp"),
            P(),
            P(),
        ),
        out_specs=(P("req", "tp"), P("req", "tp"), P("req", "tp")),
        check_vma=False,
    )
```

```python
import functools

import jax
import jax.numpy as jnp
from jax import lax
from jax.experimental import pallas as pl
from jax.experimental.pallas import tpu as pltpu
from jax.sharding import PartitionSpec as P

HEAD_DIM = 128
STATS = 128
NONE = -1e30
CHUNK = 1024
MIB = 1 << 20
LIMIT = 8
VMEM = pl.BlockSpec(memory_space=pltpu.VMEM)
ANY = pl.BlockSpec(memory_space=pl.ANY)
F32 = jnp.float32
BF16 = jnp.bfloat16


def layer_norm(values, gain_vector):
    center = jnp.mean(values, axis=-1, keepdims=True)
    shifted = values - center
    spread = jnp.mean(shifted * shifted, axis=-1, keepdims=True)
    return shifted * lax.rsqrt(spread + 1e-05) * gain_vector


def dot(a, b):
    return jnp.dot(a, b, preferred_element_type=F32)


def stream_ranges(lens_row, order_row):
    n = lens_row.shape[1]
    down = lax.broadcasted_iota(jnp.int32, (n, n), 0)
    across = lax.broadcasted_iota(jnp.int32, (n, n), 1)
    lens = lens_row.astype(F32)
    eye = down == across
    lens_col = jnp.sum(jnp.where(eye, lens, 0.0), axis=1, keepdims=True)
    holds = order_row == down
    slot_len = jnp.sum(jnp.where(holds, lens_col, 0.0), axis=0, keepdims=True)
    slot_len_col = jnp.sum(jnp.where(eye, slot_len, 0.0), axis=1, keepdims=True)
    before = jnp.sum(jnp.where(down < across, slot_len_col, 0.0), axis=0, keepdims=True)
    first = jnp.sum(jnp.where(holds, before, 0.0), axis=1, keepdims=True)
    return first.astype(jnp.int32), (first + lens_col).astype(jnp.int32)


TERM_ORDER = (10, 11, 0, 9, 2, 14, 7, 4, 5, 6, 1, 13, 15, 8, 12, 3)


def term_order(req_count, tp_count):
    n = req_count * tp_count // 2
    return TERM_ORDER if n == len(TERM_ORDER) else tuple(range(n))


def swap(x, axis, offset):
    n = lax.axis_size(axis)
    return lax.ppermute(x, axis, [(i, i ^ offset) for i in range(n)])


def far_offsets(n):
    return list(range(n - 2, 0, -2))


def exchange_order(n):
    same = [0] + far_offsets(n)
    return same + [offset + 1 for offset in same]


def gather_far(x):
    return [swap(x, "req", m) for m in far_offsets(lax.axis_size("req"))]


def gather_near(x, far):
    return [x[None]] + [part[None] for part in far] + [swap(jnp.stack([x] + far), "req", 1)]


def scatter_far(groups):
    offsets = far_offsets(lax.axis_size("req"))
    return groups[:1] + [swap(group, "req", m) for group, m in zip(groups[1:], offsets)]


def scatter_near(near, far):
    return swap(jnp.stack([near] + [part[1] for part in far]), "req", 1)


def landed_blocks(n):
    return [(c, 0) for c in range(n // 2)] + [(n // 2, c) for c in range(n // 2)]


def split_three(x):
    parts = []
    for _ in range(3):
        parts.append(x.astype(BF16).astype(F32))
        x = x - parts[-1]
    return parts


def stacked(refs):
    blocks = [ref[k].astype(F32) for ref in refs for k in range(ref.shape[0])]
    return jnp.concatenate(blocks, axis=0)


def load_kernel(n, *refs):
    sources, targets = refs[:n], refs[n : 2 * n - 2]
    bounds_ref, lens, order, sems = refs[2 * n - 2 :]
    targets = (lens, order) + targets
    copies = [
        pltpu.make_async_copy(
            source if source.shape == target.shape else source.at[pl.ds(0, target.shape[0])],
            target,
            sems.at[k],
        )
        for k, (source, target) in enumerate(zip(sources, targets))
    ]
    for copy in copies:
        copy.start()
    copies[0].wait()
    copies[1].wait()
    first, last = stream_ranges(lens[...], order[...])
    bounds_ref[0] = jnp.broadcast_to(first, bounds_ref.shape[1:])
    bounds_ref[1] = jnp.broadcast_to(last, bounds_ref.shape[1:])
    for copy in copies[2:]:
        copy.wait()


def load(lens, order, *arrays, last_rows):
    sources = [pltpu.with_memory_space_constraint(x, pltpu.HBM) for x in (lens, order) + arrays]
    last = arrays[-1]
    return pl.pallas_call(
        functools.partial(load_kernel, len(sources)),
        out_shape=[pltpu.VMEM(x.shape, x.dtype) for x in arrays[:-1]]
        + [pltpu.VMEM((last_rows, last.shape[1]), last.dtype)]
        + [pltpu.VMEM((2, lens.shape[1], 128), jnp.int32)],
        in_specs=[ANY] * len(sources),
        out_specs=[VMEM] * (len(arrays) + 1),
        scratch_shapes=[
            pltpu.VMEM(lens.shape, jnp.int32),
            pltpu.VMEM(order.shape, jnp.int32),
            pltpu.SemaphoreType.DMA((len(sources),)),
        ],
        compiler_params=pltpu.CompilerParams(vmem_limit_bytes=LIMIT * MIB),
        cost_estimate=pl.CostEstimate(
            flops=0, bytes_accessed=2 * sum(x.size for x in arrays), transcendentals=0
        ),
        name="load",
    )(*sources)


def attention_kernel(req_count, n_tokens, *refs):
    token_refs, refs = refs[:n_tokens], refs[n_tokens:]
    gain_ref, bounds, wq, first_keys, keys_hbm, values_hbm = refs[:6]
    groups = req_count // 2
    send_refs, refs = refs[6 : 6 + groups], refs[6 + groups :]
    own_normed_ref, own_queries_ref, last_keys, values, scores, sems = refs
    rows, head_width = values.shape
    held = first_keys.shape[0]
    heads = head_width // HEAD_DIM
    chunks = rows // CHUNK
    own_rows = own_normed_ref.shape[0] // 2
    requests = own_rows * req_count
    me = lax.axis_index("req")

    copies = []
    for c in range(held // CHUNK, chunks):
        there, here = pl.ds(c * CHUNK, CHUNK), pl.ds(c * CHUNK - held, CHUNK)
        copies.append(
            pltpu.make_async_copy(keys_hbm.at[there], last_keys.at[here], sems.at[len(copies)])
        )
    late = len(copies)
    for c in range(chunks):
        part = pl.ds(c * CHUNK, CHUNK)
        copies.append(
            pltpu.make_async_copy(values_hbm.at[part], values.at[part], sems.at[len(copies)])
        )
    for copy in copies:
        copy.start()
    normed = layer_norm(stacked(token_refs), gain_ref[...]).astype(BF16)
    owners = [
        pl.ds(pl.multiple_of((me ^ offset) * own_rows, own_rows), own_rows)
        for offset in exchange_order(req_count)
    ]
    first = jnp.concatenate([bounds[0, owner][:, :1] for owner in owners], axis=0) - me * rows
    last = jnp.concatenate([bounds[1, owner][:, :1] for owner in owners], axis=0) - me * rows
    queries = (dot(normed, wq[...]) * HEAD_DIM ** (-0.5)).astype(BF16)

    pairs = heads // 2
    two = 2 * requests
    wide = 2 * HEAD_DIM
    zero = jnp.zeros((requests, HEAD_DIM), BF16)
    paired = []
    for p in range(pairs):
        left = queries[:, p * wide : p * wide + HEAD_DIM]
        right = queries[:, p * wide + HEAD_DIM : (p + 1) * wide]
        upper = jnp.concatenate([left, zero], axis=1)
        lower = jnp.concatenate([zero, right], axis=1)
        paired.append(jnp.concatenate([upper, lower], axis=0))
    lane_max = [jnp.full((two, 128), NONE, F32)] * pairs
    for c in range(chunks):
        keys, at = first_keys, c * CHUNK
        if at >= held:
            copies[(at - held) // CHUNK].wait()
            keys, at = last_keys, at - held
        place = c * CHUNK + lax.broadcasted_iota(jnp.int32, (requests, CHUNK), 1)
        member = (place >= first) & (place < last)
        for p in range(pairs):
            score = lax.dot_general(
                paired[p],
                keys[at : at + CHUNK, p * wide : (p + 1) * wide],
                (((1,), (1,)), ((), ())),
                preferred_element_type=F32,
            )
            score = jnp.concatenate(
                [
                    jnp.where(member, score[:requests], NONE),
                    jnp.where(member, score[requests:], NONE),
                ],
                axis=0,
            )
            scores[p, :, c * CHUNK : (c + 1) * CHUNK] = score
            for t in range(CHUNK // 128):
                lane_max[p] = jnp.maximum(lane_max[p], score[:, t * 128 : (t + 1) * 128])

    tops = [jnp.max(lane_max[p], axis=1, keepdims=True) for p in range(pairs)]
    sums = [jnp.zeros((two, 128), F32)] * pairs
    outs = [jnp.zeros((two, wide), F32)] * pairs
    for c in range(chunks):
        copies[late + c].wait()
        for p in range(pairs):
            expo = jnp.exp(scores[p, :, c * CHUNK : (c + 1) * CHUNK] - tops[p])
            for t in range(CHUNK // 128):
                sums[p] = sums[p] + expo[:, t * 128 : (t + 1) * 128]
            outs[p] = outs[p] + dot(
                expo.astype(BF16),
                values[c * CHUNK : (c + 1) * CHUNK, p * wide : (p + 1) * wide],
            )
    peak, mass, partial = [], [], []
    for h in range(heads):
        p, r = h // 2, slice(h % 2 * requests, (h % 2 + 1) * requests)
        peak.append(tops[p][r])
        mass.append(sums[p][r])
        partial.append(outs[p][r, h % 2 * HEAD_DIM : (h % 2 + 1) * HEAD_DIM])
    lane = lax.broadcasted_iota(jnp.int32, (requests, STATS), 1)
    stats = jnp.zeros((requests, STATS), F32)
    for h in range(heads):
        both = (peak[h], jnp.sum(mass[h], axis=1, keepdims=True))
        for kind, number in enumerate(both):
            for k, piece in enumerate(split_three(number)):
                stats = jnp.where(lane == (k * 2 + kind) * heads + h, piece, stats)
    for c, ref in enumerate(send_refs):
        for k, block in enumerate((c, groups + c)):
            r = slice(block * own_rows, (block + 1) * own_rows)
            for h in range(heads):
                ref[k, :, h * HEAD_DIM : (h + 1) * HEAD_DIM] = partial[h][r].astype(BF16)
            ref[k, :, head_width : head_width + STATS] = stats[r].astype(BF16)
    own_normed_ref[...] = normed[: 2 * own_rows]
    own_queries_ref[...] = queries[: 2 * own_rows].astype(F32)


def attend(tokens, gain, bounds, wq, first_keys, keys, values):
    req_count = lax.axis_size("req")
    own_rows, width = tokens[0].shape[1:]
    requests = own_rows * req_count
    rows, head_width = keys.shape
    heads = head_width // HEAD_DIM
    groups = req_count // 2
    scratch = heads * requests * rows * 4 + 4 * rows * head_width
    *sends, own_normed, own_queries = pl.pallas_call(
        functools.partial(attention_kernel, req_count, len(tokens)),
        out_shape=[jax.ShapeDtypeStruct((2, own_rows, head_width + STATS), BF16)] * groups
        + [
            jax.ShapeDtypeStruct((2 * own_rows, width), BF16),
            jax.ShapeDtypeStruct((2 * own_rows, head_width), F32),
        ],
        in_specs=[VMEM] * (len(tokens) + 4) + [ANY] * 2,
        out_specs=[VMEM] * (groups + 2),
        scratch_shapes=[
            pltpu.VMEM((rows - first_keys.shape[0], head_width), BF16),
            pltpu.VMEM((rows, head_width), BF16),
            pltpu.VMEM((heads // 2, 2 * requests, rows), F32),
            pltpu.SemaphoreType.DMA((2 * rows // CHUNK,)),
        ],
        compiler_params=pltpu.CompilerParams(vmem_limit_bytes=scratch + LIMIT * MIB),
        name="attention",
    )(
        *tokens,
        gain,
        bounds,
        wq,
        first_keys,
        pltpu.with_memory_space_constraint(keys, pltpu.HBM),
        pltpu.with_memory_space_constraint(values, pltpu.HBM),
    )
    return sends, own_normed, own_queries


def own_kernel(normed_ref, queries_ref, wk, wv, group_ref, new_keys_ref, new_values_ref, self_ref, near_ref):
    own_rows, head_width = new_keys_ref.shape
    new_keys = dot(normed_ref[...], wk[...])[:own_rows].astype(BF16)
    new_values = dot(normed_ref[...], wv[...])[:own_rows].astype(BF16)
    new_keys_ref[...] = new_keys
    new_values_ref[...] = new_values
    product = queries_ref[:own_rows] * new_keys.astype(F32)
    lane = lax.broadcasted_iota(jnp.int32, (own_rows, STATS), 1)
    self_score = jnp.zeros((own_rows, STATS), F32)
    for h in range(head_width // HEAD_DIM):
        one = jnp.sum(product[:, h * HEAD_DIM : (h + 1) * HEAD_DIM], axis=1, keepdims=True)
        self_score = jnp.where(lane == h, one, self_score)
    self_ref[:, :head_width] = new_values.astype(F32)
    self_ref[:, head_width:] = self_score
    near_ref[...] = group_ref[1]


def own_part(normed, queries, wk, wv, group):
    own_rows, head_width = normed.shape[0] // 2, wk.shape[1]
    return pl.pallas_call(
        own_kernel,
        out_shape=[
            jax.ShapeDtypeStruct((own_rows, head_width), BF16),
            jax.ShapeDtypeStruct((own_rows, head_width), BF16),
            jax.ShapeDtypeStruct((own_rows, head_width + STATS), F32),
            jax.ShapeDtypeStruct(group.shape[1:], BF16),
        ],
        in_specs=[VMEM] * 5,
        out_specs=[VMEM] * 4,
        compiler_params=pltpu.CompilerParams(vmem_limit_bytes=LIMIT * MIB),
        name="own",
    )(normed, queries, wk, wv, group)


def merge_kernel(places, n_landed, *refs):
    landed, (self_ref, wo_ref, part_ref, sent_ref) = refs[:n_landed], refs[n_landed:]
    head_width = wo_ref.shape[0]
    heads = head_width // HEAD_DIM
    self_scores = self_ref[:, head_width:]

    def left(x, n):
        return pltpu.roll(x, STATS - n, 1)

    stats = []
    for a, k in places:
        pieces = landed[a][k, :, head_width:].astype(F32)
        stats.append(pieces + left(pieces, 2 * heads) + left(pieces, 4 * heads))
    top = functools.reduce(jnp.maximum, stats, self_scores)
    self_weight = jnp.exp(self_scores - top)
    scales = [jnp.exp(stat - top) for stat in stats]
    total = self_weight
    for stat, scale in zip(stats, scales):
        total = total + scale * left(stat, heads)
    attended = []
    for h in range(heads):
        cols = slice(h * HEAD_DIM, (h + 1) * HEAD_DIM)
        summed = self_weight[:, h : h + 1] * self_ref[:, cols]
        for (a, k), scale in zip(places, scales):
            summed = summed + scale[:, h : h + 1] * landed[a][k, :, cols].astype(F32)
        attended.append((summed / total[:, h : h + 1]).astype(BF16))
    part = dot(jnp.concatenate(attended, axis=1), wo_ref[...])
    part_ref[...] = part
    sent_ref[...] = part.astype(BF16)


def merge(landed, self_part, wo):
    shape = (self_part.shape[0], wo.shape[1])
    return pl.pallas_call(
        functools.partial(merge_kernel, landed_blocks(lax.axis_size("req")), len(landed)),
        out_shape=(jax.ShapeDtypeStruct(shape, F32), jax.ShapeDtypeStruct(shape, BF16)),
        in_specs=[VMEM] * (len(landed) + 2),
        out_specs=(VMEM,) * 2,
        compiler_params=pltpu.CompilerParams(vmem_limit_bytes=16 * MIB),
        name="merge",
    )(*landed, self_part, wo)


def middle_kernel(*refs):
    part_ref, *others, tokens_ref, gain_ref, normed_ref, columns_ref, mid = refs
    column_width = columns_ref.shape[1]
    total = part_ref[...]
    for other in others:
        total = total + other[...].astype(F32)
    middle = tokens_ref[...].astype(F32) + total
    mid[...] = middle
    normed_ref[...] = layer_norm(middle, gain_ref[...]).astype(BF16)
    offset = pl.multiple_of(lax.axis_index("tp") * column_width, column_width)
    columns_ref[...] = mid[:, pl.ds(offset, column_width)]


def middle(part, others, tokens, gain):
    own_rows, width = tokens.shape
    return pl.pallas_call(
        middle_kernel,
        out_shape=(
            jax.ShapeDtypeStruct((own_rows, width), BF16),
            jax.ShapeDtypeStruct((own_rows, width // (1 + len(others))), F32),
        ),
        in_specs=[VMEM] * (3 + len(others)),
        out_specs=(VMEM,) * 2,
        scratch_shapes=[pltpu.VMEM((own_rows, width), F32)],
        compiler_params=pltpu.CompilerParams(vmem_limit_bytes=16 * MIB),
        name="middle",
    )(part, *others, tokens, gain)


def mlp_kernel(req_count, tp_count, n_normed, *refs):
    normed_refs, (up_ref, down_ref, up_peer_ref, down_peer_ref, out_ref) = refs[:n_normed], refs[n_normed:]
    own_rows, column_width = out_ref.shape[1:]
    me = lax.axis_index("req")
    normed = stacked(normed_refs).astype(BF16)
    order = term_order(req_count, tp_count)
    activations = []
    for ref in (up_ref, up_peer_ref):
        up = dot(normed, ref[...])
        activations.append((0.5 * up * (1.0 + lax.erf(up * 0.5**0.5))).astype(BF16))
    for t in range(tp_count):
        cols = slice(t * column_width, (t + 1) * column_width)
        term = dot(activations[0], down_ref[:, cols]) + dot(activations[1], down_peer_ref[:, cols])
        for c, offset in enumerate([0] + far_offsets(req_count)):
            chip, place = (me ^ offset) // 2, 0
            for other in range(req_count // 2):
                place = jnp.where(chip == other, order.index(other * tp_count + t), place)
            out_ref[place] = term[c * own_rows : (c + 1) * own_rows].astype(BF16)


def mlp(normed, *weights):
    req_count, tp_count = lax.axis_size("req"), lax.axis_size("tp")
    own_rows, width = normed[0].shape[1:]
    return pl.pallas_call(
        functools.partial(mlp_kernel, req_count, tp_count, len(normed)),
        out_shape=jax.ShapeDtypeStruct(
            (req_count * tp_count // 2, own_rows, width // tp_count), BF16
        ),
        in_specs=[VMEM] * (len(normed) + len(weights)),
        out_specs=VMEM,
        compiler_params=pltpu.CompilerParams(vmem_limit_bytes=16 * MIB),
        name="mlp",
    )(*normed, *weights)


def finish_kernel(recv_ref, columns_ref, out_ref):
    total = recv_ref[0].astype(F32)
    for k in range(1, recv_ref.shape[0]):
        total = total + recv_ref[k].astype(F32)
    out_ref[...] = (columns_ref[...] + total).astype(BF16)


def finish(recv, columns):
    return pl.pallas_call(
        finish_kernel,
        out_shape=jax.ShapeDtypeStruct(columns.shape, BF16),
        in_specs=[VMEM] * 2,
        out_specs=VMEM,
        compiler_params=pltpu.CompilerParams(vmem_limit_bytes=16 * MIB),
        name="finish",
    )(recv, columns)


def body(
    tokens,
    first_gain,
    query_weight,
    key_weight,
    value_weight,
    out_weight,
    second_gain,
    up_weight,
    down_weight,
    cache_keys,
    cache_values,
    lengths,
    stream_order,
):
    req_count = lax.axis_size("req")
    tp_count = lax.axis_size("tp")
    up_peer, down_peer = swap(up_weight, "req", 1), swap(down_weight, "req", 1)
    far = gather_far(tokens)
    tokens, gain, wq, first_keys, bounds = load(
        lengths[None],
        stream_order[None],
        tokens,
        first_gain[None],
        query_weight,
        cache_keys,
        last_rows=cache_keys.shape[0] * 3 // 4,
    )
    sends, own_normed, own_queries = attend(
        gather_near(tokens, far), gain, bounds, wq, first_keys, cache_keys, cache_values
    )
    new_keys, new_values, self_part, near = own_part(
        own_normed, own_queries, key_weight, value_weight, sends[0]
    )
    landed = scatter_far(sends)
    landed.append(scatter_near(near, landed[1:]))
    part, sent = merge(landed, self_part, out_weight)
    others = [swap(sent, "tp", m) for m in [tp_count - 1] + list(range(1, tp_count - 1))]
    normed, columns = middle(part, others, tokens, second_gain[None])
    all_normed = [part[None] for part in [normed] + gather_far(normed)]
    term = mlp(all_normed, up_weight, down_weight, up_peer, down_peer)
    order = term_order(req_count, tp_count)
    same_core = [
        [(2 * (k // tp_count) + core) * tp_count + k % tp_count for k in order]
        for core in range(2)
    ]
    terms = lax.all_to_all(
        term,
        ("req", "tp"),
        split_axis=0,
        concat_axis=0,
        tiled=True,
        axis_index_groups=same_core,
    )
    hidden = finish(terms, columns)
    return (hidden, new_keys, new_values)


def solution(mesh):
    return jax.shard_map(
        body,
        mesh=mesh,
        in_specs=(
            P("req", None),
            P(),
            P(None, "tp"),
            P(None, "tp"),
            P(None, "tp"),
            P("tp", None),
            P(),
            P(None, ("req", "tp")),
            P(("req", "tp"), None),
            P("req", "tp"),
            P("req", "tp"),
            P(),
            P(),
        ),
        out_specs=(P("req", "tp"), P("req", "tp"), P("req", "tp")),
        check_vma=False,
    )
```
